32 devices in a mesh: req: 4 (over z), exp: 8 (over y, x, core).
Axes of the slice: x: 2, y: 2, z: 4, core: 2. Of those that a mesh axis runs over, the one named last changes fastest.
Arguments:
- hidden_in: bfloat16 [8, 512, 2048], P('exp'), may hold values from -6 to 6
- cache_keys: bfloat16 [8, 4096, 512], P('exp', None, 'req'), may hold values from -96 to 96
- cache_values: bfloat16 [8, 4096, 512], P('exp', None, 'req'), may hold values from -6 to 6
- cache_len: int32 [8], P('exp'), may hold values from 512 to 4096, as said below
- attn_gain: float32 [2048], replicated, may hold values from 0.25 to 1.75
- w_query: bfloat16 [2048, 4096], P('exp', 'req'), may hold values from -0.125 to 0.125
- w_key: bfloat16 [2048, 512], P('exp', 'req'), may hold values from -0.125 to 0.125
- w_value: bfloat16 [2048, 512], P('exp', 'req'), may hold values from -0.125 to 0.125
- q_gain: float32 [128], replicated, may hold values from 0.5 to 3
- k_gain: float32 [128], replicated, may hold values from 0.25 to 1.75
- w_out: bfloat16 [4096, 2048], P(('req', 'exp')), may hold values from -0.09375 to 0.09375
- moe_gain: float32 [2048], replicated, may hold values from 0.25 to 1.75
- expert_ids: int32 [8, 512, 8], P('exp', 'req'), may hold values from 0 to 31, all different within a row; in each aligned block of 128 rows (0 to 127, 128 to 255, ..., all dimensions but the last counted through in order) at most 48 rows name the same one
- expert_gates: float32 [8, 512, 8], P('exp', 'req'), may hold values from 0.05 to 0.5
- w_gate: bfloat16 [32, 2048, 768], P(('req', 'exp')), may hold values from -0.125 to 0.125
- w_up: bfloat16 [32, 2048, 768], P(('req', 'exp')), may hold values from -0.125 to 0.125
- w_down: bfloat16 [32, 768, 2048], P(('req', 'exp')), may hold values from -0.21875 to 0.21875
Outputs:
- hidden_out: bfloat16 [8, 512, 2048], P('exp', 'req')
- keys_out: bfloat16 [8, 4608, 512], P('exp', None, 'req')
- values_out: bfloat16 [8, 4608, 512], P('exp', None, 'req')
The draws below stay inside these ranges and needn't reach their ends.
Inputs may be any that keep to these rules, and one draw needn't show every extreme that they name: `cache_len`: some request has exactly 4096 cached entries. `expert_ids`: each token names 8 different experts. In each aligned block of 128 tokens no expert is named more than 48 times, a bound that some block reaches.
All inputs are finite; a program needn't handle non-finite values.
Results may differ from the reference program's by a relative error of at most 0.014.
Values may be sent and summed in bfloat16 or wider, within the bound.
No kernel may reach another device: no remote copies, remote signals or barrier semaphores. Data moves between devices by JAX's collectives and lax.ppermute only.
A program may use at most 128 MiB of HBM per device.

```python
import math
import jax
import jax.numpy as jnp
import numpy as np
from jax import lax

D = 2048
HEADS = 32
KVH = 4
HD = 128
FF = 768
TOP = 8
CTX = 4096
STRETCH = 512
EXPERTS = 32
REQS = 8
ROWS = 128
CAP = 48


def draw_cache_len(key, part):
    lengths = jax.random.randint(key, (REQS,), CTX // 8, CTX + 1)
    full_index = jax.random.randint(jax.random.fold_in(key, 7), (), 0, REQS)
    return jnp.where(jnp.arange(REQS) == full_index, CTX, lengths).astype(jnp.int32)


def draw_cache_keys(key, part):
    base_draw = jnp.clip(jax.random.normal(key, (REQS, CTX, KVH * HD), jnp.float32), -6.0, 6.0)
    return base_draw.astype(jnp.bfloat16)


def draw_q_gain(key, part):
    gain_vec = jnp.exp(jax.random.uniform(key, (HD,), jnp.float32, jnp.log(0.5), jnp.log(2.0)))
    return gain_vec.astype(jnp.float32)


def block_scale(stream_key, shape, cuts, smallest, top_value):
    def one(position, parts):
        heights = jax.random.uniform(jax.random.fold_in(jax.random.fold_in(stream_key, 6), position), (parts,), jnp.float32, smallest / len(cuts), top_value / len(cuts))
        return jnp.repeat(jnp.exp(heights), shape[position] // parts).reshape((-1,) + (1,) * (len(shape) - position - 1))

    level = one(*cuts[0])
    for cut in cuts[1:]:
        level = level * one(*cut)
    return level


def routed_block(own_key, own, number, rows, number_of, top, reach, slope):
    order = jax.random.permutation(own_key, number_of)
    packed, common = load_shares(number_of, rows * top, reach, slope, True), load_shares(number_of, rows * top, reach, slope, False)
    places = jnp.arange(number_of)

    def named(sizes, rotation):
        used = int((sizes > 0).sum())
        fixed = max(1, used // 4)
        moved = fixed + (places - fixed + rotation * (used - fixed)) % max(1, number_of - fixed)
        return jnp.zeros((number_of,), jnp.int32).at[order[jnp.where(places < fixed, places, moved)]].set(jnp.asarray(sizes, jnp.int32))

    sizes = jnp.where(number % 4 == 0, named(packed, number // 4), named(common, number - number // 4 - 1))
    mixed = jax.random.permutation(jax.random.fold_in(own, 3), number_of)
    giver, sink = mixed[0:number_of // 2 * 2:2], mixed[1:number_of // 2 * 2:2]
    slack = jnp.minimum(sizes[giver] - 1, reach - sizes[sink]) // 2
    slack = jnp.where((giver == order[0]) | (sink == order[0]) | (sizes[sink] == 0), 0, jnp.maximum(slack, 0))
    moved = jax.random.randint(jax.random.fold_in(own, 4), (number_of // 2,), 0, 1 << 20) % (slack + 1)
    sizes = sizes.at[giver].add(-moved).at[sink].add(moved)
    labels = jnp.searchsorted(jnp.cumsum(sizes), jnp.arange(rows * top), side="right").astype(jnp.int32)
    table = labels.reshape(top, rows).T
    table = table[jax.random.permutation(jax.random.fold_in(own, 1), rows)]
    rotation = jax.random.randint(jax.random.fold_in(own, 2), (rows, 1), 0, top)
    return jnp.take_along_axis(table, (jnp.arange(top)[None, :] + rotation) % top, axis=1)


def load_shares(number_of, total, reach, skew, full):
    loads = [(1 << 20) // math.isqrt(grade ** skew) + 1 for grade in range(1, number_of + 1)]
    largest = reach if full else min(reach, max(-(-total // number_of), total * loads[0] // sum(loads)))
    least = 1 if total - largest >= number_of - 1 else 0
    given, rest = [largest] + [least] * (number_of - 1), total - largest - least * (number_of - 1)
    while rest > 0:
        candidates = [i for i in range(1, number_of) if given[i] < largest] or [i for i in range(1, number_of) if given[i] < reach]
        whole, budget = sum([loads[i] for i in candidates]), rest
        for i in candidates:
            addition = min(reach - given[i], max(1, budget * loads[i] // whole), rest)
            given[i] = given[i] + addition
            rest = rest - addition
    return np.array(given)


def normal_values(stream_key, dims, width, limit, shards=(), held_as=jnp.bfloat16):
    factor_of = block_scale(stream_key, dims, shards, -0.22, 0.18) if shards else 1.0
    drawn = jax.random.normal(stream_key, dims, jnp.float32) * width * factor_of
    return jnp.minimum(jnp.maximum(drawn, -limit), limit).astype(held_as)


def setup_inputs(seed: int = 0) -> dict:
    seeds = jax.random.split(jax.random.key(seed), 18)
    hidden_in = normal_values(seeds[0], (REQS, STRETCH, D), 1.0, 6.0, ((0, 8),))
    cache_keys = draw_cache_keys(jax.random.fold_in(seeds[17], 71), 0)
    cache_values = normal_values(seeds[2], (REQS, CTX, KVH * HD), 1.0, 6.0, ((0, 8), (2, 4)))
    cache_len = draw_cache_len(jax.random.fold_in(seeds[17], 71), 0)
    attn_gain = jnp.clip(1.0 + 0.15 * jax.random.normal(seeds[4], (D,), jnp.float32), 0.25, 1.75)
    w_query = normal_values(seeds[5], (D, HEADS * HD), D ** -0.5, 0.125, ((0, 8), (1, 4)))
    w_key = normal_values(seeds[6], (D, KVH * HD), D ** -0.5, 0.125, ((0, 8), (1, 4)))
    w_value = normal_values(seeds[7], (D, KVH * HD), D ** -0.5, 0.125, ((0, 8), (1, 4)))
    q_gain = draw_q_gain(jax.random.fold_in(seeds[17], 71), 0)
    k_gain = jnp.clip(1.0 + 0.15 * jax.random.normal(seeds[9], (HD,), jnp.float32), 0.25, 1.75)
    w_out = normal_values(seeds[10], (HEADS * HD, D), (HEADS * HD) ** -0.5, 0.09375, ((0, 32),))
    moe_gain = jnp.clip(1.0 + 0.15 * jax.random.normal(seeds[11], (D,), jnp.float32), 0.25, 1.75)
    expert_ids_keys = jax.random.split(jax.random.fold_in(seeds[12], 1), REQS * STRETCH // ROWS)
    expert_ids_turns = jax.random.permutation(jax.random.fold_in(seeds[12], 3), REQS * STRETCH // ROWS)
    expert_ids = jax.vmap(lambda own, number: routed_block(jax.random.fold_in(seeds[12], 2), own, number, ROWS, EXPERTS, TOP, CAP, 2))(expert_ids_keys, expert_ids_turns).reshape((REQS, STRETCH, TOP))
    expert_gates = jnp.clip(jnp.exp(math.log(0.5) - 2.3025851 * jax.random.uniform(seeds[13], (REQS, STRETCH, TOP), jnp.float32) ** block_scale(seeds[13], (REQS, STRETCH, TOP), ((0, 8), (1, 4)), -0.2, 0.2)), 0.05, 0.5)
    w_gate = normal_values(seeds[14], (EXPERTS, D, FF), D ** -0.5, 0.125, ((0, 32),))
    w_up = normal_values(seeds[15], (EXPERTS, D, FF), D ** -0.5, 0.125, ((0, 32),))
    w_down = normal_values(seeds[16], (EXPERTS, FF, D), FF ** -0.5, 0.21875, ((0, 32),))
    return {"hidden_in": hidden_in, "cache_keys": cache_keys, "cache_values": cache_values, "cache_len": cache_len, "attn_gain": attn_gain, "w_query": w_query, "w_key": w_key, "w_value": w_value, "q_gain": q_gain, "k_gain": k_gain, "w_out": w_out, "moe_gain": moe_gain, "expert_ids": expert_ids, "expert_gates": expert_gates, "w_gate": w_gate, "w_up": w_up, "w_down": w_down}


EPS = 1e-06
THETA = 1000000.0

def rms_norm(values, gain_vec):
    values = values.astype(jnp.float32)
    factor = lax.rsqrt(lax.optimization_barrier(jnp.mean(values * values, axis=-1, keepdims=True)) + EPS)
    return values * factor * gain_vec.astype(jnp.float32)

def rotate(values, positions):
    half_dim = values.shape[-1] // 2
    frequency = THETA ** (-jnp.arange(half_dim, dtype=jnp.float32) * 2.0 / values.shape[-1])
    angles = positions.astype(jnp.float32)[:, None] * frequency[None, :]
    cosine = jnp.cos(angles)[:, None, :]
    sine_part = jnp.sin(angles)[:, None, :]
    lower_half = values[..., :half_dim]
    upper_half = values[..., half_dim:]
    return jnp.concatenate([lower_half * cosine - upper_half * sine_part, upper_half * cosine + lower_half * sine_part], axis=-1)

def finish(query_proj, key_proj, value_proj, q_gain, k_gain, positions):
    stretch_len = query_proj.shape[0]
    head_dim = q_gain.shape[0]
    queries = rotate(rms_norm(query_proj.reshape(stretch_len, -1, head_dim), q_gain), positions).astype(jnp.bfloat16)
    fresh_keys = rotate(rms_norm(key_proj.reshape(stretch_len, -1, head_dim), k_gain), positions).astype(jnp.bfloat16)
    return (queries.transpose(1, 0, 2), fresh_keys.reshape(stretch_len, -1), value_proj.astype(jnp.bfloat16))

def context(cache, fresh, head_dim):
    joined = jnp.concatenate([cache, fresh], axis=0)
    return joined.reshape(joined.shape[0], -1, head_dim).transpose(1, 0, 2)

def visible(length, context_len, stretch_len):
    key_pos = jnp.arange(context_len + stretch_len, dtype=jnp.int32)[None, :]
    query_pos = jnp.arange(stretch_len, dtype=jnp.int32)[:, None]
    return (key_pos < length) | (key_pos >= context_len) & (key_pos - context_len <= query_pos)

def attend(queries, keys, values, visible_mask):
    group_size = queries.shape[0] // keys.shape[0]
    score_scale = queries.shape[2] ** (-0.5)

    def one_head(operands):
        query_head, head_index = operands
        key_block = keys[head_index // group_size]
        value_block = values[head_index // group_size]
        scores = jnp.dot(query_head, key_block.T, preferred_element_type=jnp.float32) * score_scale
        scores = jnp.where(visible_mask, scores, -1e+30)
        row_peak = lax.optimization_barrier(jnp.max(scores, axis=1, keepdims=True))
        weights = jnp.where(visible_mask, jnp.exp(scores - row_peak), 0.0)
        running = lax.optimization_barrier(jnp.sum(weights, axis=1, keepdims=True))
        mixed = jnp.dot(weights.astype(jnp.bfloat16), value_block, preferred_element_type=jnp.float32)
        return (mixed / running).astype(jnp.bfloat16)
    return lax.map(one_head, (queries, jnp.arange(queries.shape[0], dtype=jnp.int32)))

def append(cache, fresh, length):
    span = cache.shape[0] + fresh.shape[0]
    padded = jnp.concatenate([cache, jnp.zeros_like(fresh)], axis=0)
    kept_rows = jnp.where((jnp.arange(span, dtype=jnp.int32) < length)[:, None], padded, jnp.zeros_like(padded))
    return lax.dynamic_update_slice(kept_rows, fresh, (length.astype(jnp.int32), jnp.zeros((), jnp.int32)))

def reference(hidden_in, cache_keys, cache_values, cache_len, attn_gain, w_query, w_key, w_value, q_gain, k_gain, w_out, moe_gain, expert_ids, expert_gates, w_gate, w_up, w_down):

    def per_request(operands):
        tokens, cache_k, cache_v, length = operands
        normed = rms_norm(tokens, attn_gain).astype(jnp.bfloat16)
        positions = length + jnp.arange(STRETCH, dtype=jnp.int32)
        queries, fresh_keys, fresh_values = finish(jnp.dot(normed, w_query, preferred_element_type=jnp.float32), jnp.dot(normed, w_key, preferred_element_type=jnp.float32), jnp.dot(normed, w_value, preferred_element_type=jnp.float32), q_gain, k_gain, positions)
        visible_mask = visible(length, CTX, STRETCH)
        attended = attend(queries, context(cache_k, fresh_keys, HD), context(cache_v, fresh_values, HD), visible_mask)
        attended = attended.transpose(1, 0, 2).reshape(STRETCH, HEADS * HD)
        mixed = jnp.dot(attended, w_out, preferred_element_type=jnp.float32)
        after_attn = (tokens.astype(jnp.float32) + mixed).astype(jnp.bfloat16)
        return (after_attn, append(cache_k, fresh_keys, length), append(cache_v, fresh_values, length))
    after_attn, keys_out, values_out = lax.map(per_request, (hidden_in, cache_keys, cache_values, cache_len))
    tokens_all = after_attn.reshape(-1, D)
    moe_in = rms_norm(tokens_all, moe_gain).astype(jnp.bfloat16)
    flat_ids = expert_ids.reshape(-1).astype(jnp.int32)
    flat_gates = expert_gates.reshape(-1).astype(jnp.float32)
    pair_order = jnp.argsort(flat_ids, stable=True).astype(jnp.int32)
    counts = jax.ops.segment_sum(jnp.ones_like(flat_ids), flat_ids, num_segments=EXPERTS).astype(jnp.int32)
    starts = (jnp.cumsum(counts) - counts).astype(jnp.int32)
    slot_count = EXPERTS * CAP
    pair_order = jnp.concatenate([pair_order, jnp.zeros((slot_count,), jnp.int32)])

    def serve_rows(accumulated, expert):
        picked = lax.dynamic_slice(pair_order, (starts[expert],), (slot_count,))
        live_slot = jnp.arange(slot_count, dtype=jnp.int32) < counts[expert]
        token_rows = picked // TOP
        block_in = moe_in[token_rows]
        gate_proj = jnp.dot(block_in, w_gate[expert], preferred_element_type=jnp.float32)
        up_proj = jnp.dot(block_in, w_up[expert], preferred_element_type=jnp.float32)
        activated = (jax.nn.silu(gate_proj) * up_proj).astype(jnp.bfloat16)
        produced = jnp.dot(activated, w_down[expert], preferred_element_type=jnp.float32).astype(jnp.bfloat16)
        weight = jnp.where(live_slot, flat_gates[picked], 0.0)
        return (accumulated.at[token_rows].add(produced.astype(jnp.float32) * weight[:, None]), None)
    accumulated, _ = lax.scan(serve_rows, jnp.zeros(tokens_all.shape, jnp.float32), jnp.arange(EXPERTS, dtype=jnp.int32))
    hidden_out = (tokens_all.astype(jnp.float32) + accumulated).astype(jnp.bfloat16).reshape(REQS, STRETCH, D)
    return (hidden_out, keys_out, values_out)
```

```python
import functools
import math

import jax
import jax.numpy as jnp
from jax import lax
from jax.experimental import pallas as pl
from jax.experimental.pallas import tpu as pltpu
from jax.sharding import PartitionSpec as P

EPS = 1e-06
THETA = 1000000.0
ROWS = 128
ORDER = (0, 2, 1, 3)
HIDE = -1e30
KEYS = 512
TILE = 256
PICK = 384
CHUNKS = (64, 64)
WIDE = 1024
MB = 1024 * 1024
F32 = jnp.float32
BF16 = jnp.bfloat16

VMEM = pltpu.VMEM
SMEM = pltpu.SMEM
HBM = pltpu.HBM


def spec(space):
    return pl.BlockSpec(memory_space=space)


def params(limit_mb):
    return pltpu.CompilerParams(vmem_limit_bytes=limit_mb * MB)


def swap(value, bit, size):
    return lax.ppermute(value, "exp", [(i, i ^ bit) for i in range(size)])


def shift(value, step, size):
    return lax.ppermute(value, "req", [(i, (i + step) % size) for i in range(size)])


def chip_bits(size):
    bits, bit = [], 2
    while bit < size:
        bits.append(bit)
        bit *= 2
    return bits


def spread(value, size):
    half = value.shape[0] // 2
    if size == 8:
        x, y = swap(value, 2, size), swap(value, 4, size)
        first, second = swap(x[:half], 4, size), swap(y[half:], 2, size)
        out = [(0, 0, value), (2, 0, x), (4, 0, y), (6, 0, first), (6, half, second)]
    else:
        out = []
        for start in (0, half):
            held = {0: value[start : start + half]}
            for bit in chip_bits(size) if start == 0 else chip_bits(size)[::-1]:
                held.update({b ^ bit: swap(v, bit, size) for b, v in list(held.items())})
            out += [(b, start, v) for b, v in held.items()]
    return out + [(b ^ 1, start, swap(v, 1, size)) for b, start, v in out]


def add(*terms):
    total = terms[0].astype(F32)
    for term in terms[1:]:
        total = total + term.astype(F32)
    return total.astype(BF16)


def gather_sums(parts, size):
    half = parts[0].shape[0] // 2
    both = {b: (parts[b], swap(parts[b ^ 1], 1, size)) for b in (6, 4, 2, 0)}
    first = add(*(v[:half] for v in both[6]))
    second = add(*(v[half:] for v in both[6]))
    first, second = swap(first, 2, size), swap(second, 4, size)
    y = jnp.concatenate([add(*(v[:half] for v in both[4]), first), add(*(v[half:] for v in both[4]))])
    x = jnp.concatenate([add(*(v[:half] for v in both[2])), add(*(v[half:] for v in both[2]), second)])
    return both[0] + (swap(x, 2, size), swap(y, 4, size)), [v[1] for v in both.values()]


def along(value, pairs):
    return lax.ppermute(value, "req", pairs)


def along_sum(parts, z, groups):
    if groups != 4:
        return [parts[0]] + [shift(parts[k], k, groups) for k in range(1, groups)]
    up = along(parts[1], [(0, 1), (1, 2), (2, 3)])
    down = along(parts[3], [(1, 0), (2, 1), (3, 2)])
    relayed = along(parts[4], [(0, 1), (3, 2)])
    over = along(add(parts[2], relayed), [(0, 2), (1, 3), (2, 0), (3, 1)])
    return [parts[0], up, down, over]


def along_gather(value, z, groups):
    over = along(value, [(0, 2), (1, 3), (2, 0), (3, 1)])
    up = along(value, [(0, 1), (1, 2), (2, 3)])
    down = along(value, [(1, 0), (2, 1), (3, 2)])
    relayed = along(over, [(1, 0), (2, 3)])
    got = [value, jnp.where(z == 0, relayed, up), over, jnp.where(z == 3, relayed, down)]
    return jnp.concatenate([got[k] for k in ORDER])


def stage_kernel(w_ref, *rest):
    rest[-1][...] = w_ref[...]


def stage(w, extra):
    return pl.pallas_call(
        stage_kernel,
        out_shape=jax.ShapeDtypeStruct(w.shape, w.dtype),
        in_specs=[spec(VMEM)] + [spec(HBM)] * len(extra),
        out_specs=spec(VMEM),
        name="stage",
    )(w, *extra)


def start_loads(e, pieces, at, shard, w_ref, sem):
    copies = []
    for i, (piece, (b, start)) in enumerate(zip(pieces, at)):
        row = pl.multiple_of((e ^ b) * shard + start, 16)
        copy = pltpu.make_async_copy(piece, w_ref.at[pl.ds(row, piece.shape[0])], sem.at[i])
        copy.start()
        copies.append(copy)
    return copies


def project_kernel(marks, x_ref, gain_ref, cos_ref, sin_ref, qg_ref, kg_ref, *rest, at, shard, heads, chunks, groups):
    pieces, rest = rest[: len(at)], rest[len(at) :]
    q_refs, rest = rest[: len(chunks)], rest[len(chunks) :]
    k_ref, v_ref, w_ref, n_ref, sem = rest
    copies = start_loads(marks[1], pieces, at, shard, w_ref, sem)
    x = x_ref[...].astype(F32)
    factor = lax.rsqrt(jnp.mean(x * x, axis=-1, keepdims=True) + EPS)
    n_ref[...] = (x * factor * gain_ref[...]).astype(BF16)
    for copy in copies:
        copy.wait()
    hd = qg_ref.shape[1]
    starts = [sum(chunks[:c]) for c in range(len(chunks))]

    def turned(value, gain):
        factor = lax.rsqrt(jnp.mean(value * value, axis=-1, keepdims=True) + EPS)
        value = value * factor * gain
        return value * cos_ref[...] + pltpu.roll(value, hd // 2, 1) * sin_ref[...]

    scale = hd ** (-0.5) * math.log2(math.e)

    for first in range(0, heads, 4):
        four = jnp.dot(n_ref[...], w_ref[:, first * hd : (first + 4) * hd], preferred_element_type=F32)
        for s in range(4):
            q = (turned(four[:, s * hd : (s + 1) * hd], qg_ref[...]) * scale).astype(BF16)
            for c, rows in enumerate(chunks):
                span = groups * rows
                q_refs[c][(first + s) * span : (first + s + 1) * span] = q[starts[c] * groups :][:span]
    both = jnp.dot(n_ref[...], w_ref[:, heads * hd : (heads + 2) * hd], preferred_element_type=F32)
    k = turned(both[:, :hd], kg_ref[...]).astype(BF16)
    v = both[:, hd:].astype(BF16)
    for c, rows in enumerate(chunks):
        for r in range(groups):
            src = slice(starts[c] * groups + r * rows, starts[c] * groups + (r + 1) * rows)
            dst = slice(r * ROWS + starts[c], r * ROWS + starts[c] + rows)
            k_ref[dst] = k[src]
            v_ref[dst] = v[src]


def project(marks, x, gain, cos, sin, q_gain, k_gain, pieces, size, heads, chunks, groups):
    tokens, width = x.shape
    hd = q_gain.shape[1]
    at = [piece[:2] for piece in pieces]
    pieces = [piece[2] for piece in pieces]
    cols = pieces[0].shape[1]
    return pl.pallas_call(
        functools.partial(project_kernel, at=at, shard=width // size, heads=heads, chunks=chunks, groups=groups),
        out_shape=(
            *(jax.ShapeDtypeStruct((heads * groups * rows, hd), BF16) for rows in chunks),
            jax.ShapeDtypeStruct((tokens, hd), BF16),
            jax.ShapeDtypeStruct((tokens, hd), BF16),
        ),
        in_specs=[spec(SMEM)] + [spec(VMEM)] * 6 + [spec(HBM)] * len(pieces),
        out_specs=(spec(VMEM),) * (2 + len(chunks)),
        scratch_shapes=[
            VMEM((width, cols), BF16),
            VMEM((tokens, width), BF16),
            pltpu.SemaphoreType.DMA((len(pieces),)),
        ],
        compiler_params=params(40),
        cost_estimate=pl.CostEstimate(flops=2 * tokens * width * cols, bytes_accessed=10 * MB, transcendentals=0),
        name="project",
    )(marks, x, gain, cos, sin, q_gain, k_gain, *pieces)


def attend_kernel(marks, q_hbm, kc_hbm, vc_hbm, kn_hbm, vn_hbm, *rest, start, rows, heads):
    o_ref, marks_out, qa, ka, va, s0, s1, m0, m1, bias, sem = rest[-11:]
    ctx, hd = kc_hbm.shape
    keys = ctx + kn_hbm.shape[0]
    tokens = qa.shape[0] // heads
    loads = [
        pltpu.make_async_copy(src, dst, sem.at[i])
        for i, (src, dst) in enumerate(
            (
                (q_hbm, qa.at[:, :hd]),
                (kc_hbm, ka.at[:ctx, :hd]),
                (kn_hbm, ka.at[ctx:, :hd]),
                (vc_hbm, va.at[:ctx, :hd]),
                (vn_hbm, va.at[ctx:, :hd]),
            )
        )
    ]
    for load in loads:
        load.start()
    for i in range(3):
        marks_out[i] = marks[i]
    length = marks[0]
    lane = lax.broadcasted_iota(jnp.int32, (1, hd), 1)
    qa[:, hd:] = jnp.broadcast_to(jnp.where(lane == 0, 1.0, 0.0), (heads * tokens, hd)).astype(BF16)
    where = lax.broadcasted_iota(jnp.int32, (keys, hd), 0)
    first = lax.broadcasted_iota(jnp.int32, (keys, hd), 1) == 0
    ka[:, hd:] = jnp.where(first & (where >= length) & (where < ctx), HIDE, 0.0).astype(BF16)
    va[:, hd:] = jnp.ones((keys, hd), BF16)
    tile = bias.shape[0]
    at = lax.broadcasted_iota(jnp.int32, (tile, KEYS), 0) % tokens
    token = (at // rows) * ROWS + start + at % rows
    bias[...] = jnp.where(lax.broadcasted_iota(jnp.int32, (tile, KEYS), 1) <= token, 0.0, HIDE)
    blocks = keys // KEYS
    tiles = heads * tokens // tile
    per = tile // tokens

    for load in loads:
        load.wait()

    def scores(i, buf, j, peak):
        q = qa[pl.ds(pl.multiple_of(i * tile, tile), tile)]
        s = lax.dot_general(q, ka[j * KEYS : (j + 1) * KEYS], (((1,), (1,)), ((), ())), preferred_element_type=F32)
        if j == blocks - 1:
            s = s + bias[...]
        buf[:, j * KEYS : (j + 1) * KEYS] = s
        for c in range(KEYS // hd):
            part = s[:, c * hd : (c + 1) * hd]
            peak = part if peak is None else jnp.maximum(peak, part)
        return peak

    def top(peak):
        return jnp.broadcast_to(jnp.max(peak, axis=1, keepdims=True), (tile, hd))

    def mix(buf, m_ref, j, total):
        m = m_ref[...]
        s = buf[:, j * KEYS : (j + 1) * KEYS]
        p = jnp.concatenate(
            [jnp.exp2(s[:, c * hd : (c + 1) * hd] - m).astype(BF16) for c in range(KEYS // hd)], axis=1
        )
        part = jnp.dot(p, va[j * KEYS : (j + 1) * KEYS], preferred_element_type=F32)
        return part if total is None else total + part

    def finish(i, total):
        out = (total[:, :hd] / total[:, hd:]).astype(BF16)
        for h in range(per):
            o_ref[i * per + h] = out[h * tokens : (h + 1) * tokens]

    bufs, peaks = (s0, s1), (m0, m1)

    def step(i, parity, score, mixing):
        peak = total = None
        for j in range(blocks):
            if score:
                peak = scores(i, bufs[parity], j, peak)
            if mixing:
                total = mix(bufs[1 - parity], peaks[1 - parity], j, total)
        if score:
            peaks[parity][...] = top(peak)
        if mixing:
            finish(i - 1, total)

    step(0, 0, True, False)
    step(1, 1, True, True)

    def two(n, carry):
        step(2 * n, 0, True, True)
        step(2 * n + 1, 1, True, True)
        return carry

    lax.fori_loop(1, tiles // 2, two, 0)
    step(tiles, 0, False, True)


def attend(marks, q, kc, vc, kn, vn, start, rows, heads, extra=()):
    hd = q.shape[1]
    tokens = q.shape[0] // heads
    keys = kc.shape[0] + kn.shape[0]
    tile = tokens * max(1, TILE // tokens)
    return pl.pallas_call(
        functools.partial(attend_kernel, start=start, rows=rows, heads=heads),
        out_shape=(jax.ShapeDtypeStruct((heads, tokens, hd), BF16), jax.ShapeDtypeStruct((3,), jnp.int32)),
        in_specs=[spec(SMEM)] + [spec(HBM)] * (5 + len(extra)),
        out_specs=(spec(VMEM), spec(SMEM)),
        scratch_shapes=[
            VMEM((heads * tokens, 2 * hd), BF16),
            VMEM((keys, 2 * hd), BF16),
            VMEM((keys, 2 * hd), BF16),
            VMEM((tile, keys), F32),
            VMEM((tile, keys), F32),
            VMEM((tile, hd), F32),
            VMEM((tile, hd), F32),
            VMEM((tile, KEYS), F32),
            pltpu.SemaphoreType.DMA((5,)),
        ],
        compiler_params=params(40),
        cost_estimate=pl.CostEstimate(
            flops=8 * heads * tokens * keys * hd, bytes_accessed=4 * MB, transcendentals=heads * tokens * keys
        ),
        name="attend",
    )(marks, q, kc, vc, kn, vn, *extra)


def out_kernel(marks, att_ref, *rest, at, shard, groups):
    pieces, rest = rest[: len(at)], rest[len(at) :]
    outs, (w_ref, o_ref, sem) = rest[:-3], rest[-3:]
    copies = start_loads(marks[1], pieces, at, shard, w_ref, sem)
    heads, tokens, hd = att_ref.shape
    att = jnp.concatenate([att_ref[h] for h in range(heads)], axis=1)
    for copy in copies:
        copy.wait()
    rows = tokens // groups

    for n in range(0, w_ref.shape[1], WIDE):
        cols = slice(n, n + WIDE)
        part = jnp.dot(att, w_ref[:, cols], preferred_element_type=F32).astype(BF16)
        for r in range(groups):
            o_ref[r, :, cols] = part[r * rows : (r + 1) * rows]
    for k in range(groups):
        outs[k][...] = o_ref[lax.rem(marks[2] + k, groups)]
    outs[groups][...] = o_ref[jnp.where(marks[2] == 0, groups - 1, 0)]


def out_project(marks, att, pieces, size, groups):
    heads, tokens, hd = att.shape
    at = [piece[:2] for piece in pieces]
    pieces = [piece[2] for piece in pieces]
    width = pieces[0].shape[1]
    rows = tokens // groups
    return pl.pallas_call(
        functools.partial(out_kernel, at=at, shard=heads * hd // size, groups=groups),
        out_shape=(jax.ShapeDtypeStruct((rows, width), BF16),) * (groups + 1),
        in_specs=[spec(SMEM), spec(VMEM)] + [spec(HBM)] * len(pieces),
        out_specs=(spec(VMEM),) * (groups + 1),
        scratch_shapes=[
            VMEM((heads * hd, width), BF16),
            VMEM((groups, rows, width), BF16),
            pltpu.SemaphoreType.DMA((len(pieces),)),
        ],
        compiler_params=params(24),
        cost_estimate=pl.CostEstimate(flops=2 * tokens * heads * hd * width, bytes_accessed=5 * MB, transcendentals=0),
        name="out_project",
    )(marks, att, *pieces)


def norm_kernel(x_ref, gain_ref, *rest):
    parts, (after_ref, moe_ref) = rest[:-2], rest[-2:]
    total = parts[0][...].astype(F32)
    for part in parts[1:]:
        total = total + part[...].astype(F32)
    after = (x_ref[...].astype(F32) + total).astype(BF16)
    after_ref[...] = after
    x = after.astype(F32)
    factor = lax.rsqrt(jnp.mean(x * x, axis=-1, keepdims=True) + EPS)
    moe_ref[...] = (x * factor * gain_ref[...]).astype(BF16)


def add_norm(x, gain, parts):
    shape = jax.ShapeDtypeStruct(x.shape, BF16)
    return pl.pallas_call(
        norm_kernel,
        out_shape=(shape, shape),
        in_specs=[spec(VMEM)] * (2 + len(parts)),
        out_specs=(spec(VMEM),) * 2,
        name="add_norm",
    )(x, gain, *parts)


def expert_kernel(count_ref, slot_ref, gate_ref, *rest, at, span, extras):
    pieces, rest = rest[: len(at)], rest[len(at) :]
    wg_hbm, wu_hbm, wd_hbm = rest[:3]
    outs = rest[3 + extras : -8]
    x_ref, wg, wu, wd, xg, hid, sem, wsem = rest[-8:]
    copies = []
    for i, (piece, (b, start)) in enumerate(zip(pieces, at)):
        row = b * span + start
        copy = pltpu.make_async_copy(piece, x_ref.at[row : row + piece.shape[0]], sem.at[i])
        copy.start()
        copies.append(copy)
    loads = []
    for i, (src, dst) in enumerate(((wg_hbm, wg), (wu_hbm, wu), (wd_hbm, wd))):
        copy = pltpu.make_async_copy(src, dst, wsem.at[i])
        copy.start()
        loads.append(copy)
    tokens, width = x_ref.shape
    slots = slot_ref[...]
    slots_t = jnp.transpose(jnp.broadcast_to(slots, (128, tokens)))

    def tile(base, first):
        slot = lax.broadcasted_iota(jnp.int32, (PICK, tokens), 0).astype(F32) + base
        hit = slot == slots
        pick = jnp.where(hit, 1.0, 0.0).astype(BF16)
        gate = jnp.sum(jnp.where(hit, gate_ref[...], 0.0), axis=1, keepdims=True)
        lane = lax.broadcasted_iota(jnp.int32, (tokens, 128), 1).astype(F32) + base
        put = jnp.concatenate(
            [jnp.where(lane + n == slots_t, 1.0, 0.0).astype(BF16) for n in range(0, PICK, 128)], axis=1
        )
        if first:
            for copy in copies:
                copy.wait()
        for n in range(0, width, WIDE):
            cols = slice(n, n + WIDE)
            xg[:, cols] = jnp.dot(pick, x_ref[:, cols], preferred_element_type=F32).astype(BF16)
        if first:
            loads[0].wait()
            loads[1].wait()
        g = jnp.dot(xg[...], wg[...], preferred_element_type=F32)
        u = jnp.dot(xg[...], wu[...], preferred_element_type=F32)
        hid[...] = (g / (1.0 + jnp.exp(-g)) * u).astype(BF16)
        if first:
            loads[2].wait()
        for n in range(0, width, WIDE):
            cols = slice(n, n + WIDE)
            o = jnp.dot(hid[...], wd[:, cols], preferred_element_type=F32).astype(BF16)
            o = (o.astype(F32) * gate).astype(BF16)
            back = jnp.dot(put, o, preferred_element_type=F32).astype(BF16)
            for i, out in enumerate(outs):
                part = back[i * span : (i + 1) * span]
                out[:, cols] = part if first else out[:, cols] + part

    tile(0.0, True)

    def more(i, carry):
        tile((i * PICK).astype(F32), False)
        return carry

    lax.fori_loop(1, lax.div(count_ref[0] + (PICK - 1), PICK), more, 0)


def experts(count, slots, gate, pieces, wg, wu, wd, extra, size):
    at = [piece[:2] for piece in pieces]
    pieces = [piece[2] for piece in pieces]
    span, width = pieces[0].shape
    tokens = size * span
    n = len(pieces)
    ff = wg.shape[1]
    return pl.pallas_call(
        functools.partial(expert_kernel, at=at, span=span, extras=len(extra)),
        out_shape=(jax.ShapeDtypeStruct((span, width), BF16),) * size,
        in_specs=[spec(SMEM)] + [spec(VMEM)] * 2 + [spec(HBM)] * (n + 3 + len(extra)),
        out_specs=(spec(VMEM),) * size,
        scratch_shapes=[
            VMEM((tokens, width), BF16),
            VMEM(wg.shape, BF16),
            VMEM(wu.shape, BF16),
            VMEM(wd.shape, BF16),
            VMEM((PICK, width), BF16),
            VMEM((PICK, ff), BF16),
            pltpu.SemaphoreType.DMA((n,)),
            pltpu.SemaphoreType.DMA((3,)),
        ],
        compiler_params=params(48),
        cost_estimate=pl.CostEstimate(
            flops=6 * PICK * width * ff + 4 * PICK * tokens * width, bytes_accessed=18 * MB, transcendentals=0
        ),
        name="experts",
    )(count, slots, gate, *pieces, wg, wu, wd, *extra)


def by_gathers(tokens, gates_to_me, moe_gain, w_gate, w_up, w_down, groups, size, chunks, head_parts):
    z = lax.axis_index("req")
    resident = lax.dynamic_slice_in_dim(tokens, z * ROWS, ROWS, 0)
    starts = [sum(chunks[:c]) for c in range(len(chunks))]
    done = []
    for c, rows in enumerate(chunks):
        parts, marks = head_parts(c)
        if c == 0:
            near = jnp.arange(size, dtype=jnp.int32)[:, None] ^ marks[1]
            far = (marks[2] - jnp.array(ORDER, jnp.int32)[None]) % groups
            near_first = gates_to_me[(far * size + near).reshape(-1)]
        after, moe_in = add_norm(resident[starts[c] : starts[c] + rows], moe_gain[None], along_sum(parts, z, groups))
        done.append((after, along_gather(moe_in, z, groups)))
    last, results = [], []
    for c, rows in enumerate(chunks):
        after, stack = done[c]
        mine = near_first[:, starts[c] : starts[c] + rows].reshape(1, -1)
        at = jnp.arange(mine.shape[1], dtype=jnp.int32)
        routed = mine > 0
        before = jnp.dot(routed.astype(BF16), (at[:, None] < at[None, :]).astype(BF16), preferred_element_type=F32)
        slots = jnp.where(routed, before, -1.0)
        count = jnp.sum(routed.astype(jnp.int32), axis=1)
        made = experts(count, slots, mine, spread(stack, size), w_gate, w_up, w_down, last, size)
        terms, last = gather_sums(made, size)
        cut = {k: add(*(term[i * rows : (i + 1) * rows] for term in terms)) for i, k in enumerate(ORDER)}
        edge = jnp.where(z == 0, cut[1], cut[3])
        parts = along_sum([cut[0], cut[3], cut[2], cut[1], edge], z, groups)
        results.append(add(after, *parts))
    return jnp.concatenate(results), marks[0]


def by_all_to_all(routes, gates, after_attn, moe_in, w_gate, w_up, w_down, experts_n):
    row_count, model_width = moe_in.shape
    top_k = routes.shape[1]
    capacity = 3 * top_k * row_count // (2 * experts_n)
    flat_ids = routes.reshape(-1)
    onehot = (flat_ids[:, None] == jnp.arange(experts_n, dtype=jnp.int32)[None, :]).astype(jnp.int32)
    slots = jnp.sum((jnp.cumsum(onehot, axis=0) - 1) * onehot, axis=1)
    target = flat_ids * capacity + slots
    sources = jnp.arange(row_count * top_k, dtype=jnp.int32) // top_k
    outgoing = jnp.zeros((experts_n * capacity, model_width), BF16).at[target].set(moe_in[sources])
    outgoing = outgoing.reshape(experts_n, capacity, model_width)
    block_in = lax.all_to_all(outgoing, ("req", "exp"), split_axis=0, concat_axis=0, tiled=True)
    flat_rows = block_in.reshape(-1, model_width)
    gate_proj = jnp.dot(flat_rows, w_gate, preferred_element_type=F32)
    up_proj = jnp.dot(flat_rows, w_up, preferred_element_type=F32)
    activated = (jax.nn.silu(gate_proj) * up_proj).astype(BF16)
    produced = jnp.dot(activated, w_down, preferred_element_type=F32).astype(BF16)
    returned = lax.all_to_all(
        produced.reshape(block_in.shape), ("req", "exp"), split_axis=0, concat_axis=0, tiled=True
    )
    picked = returned.reshape(experts_n * capacity, model_width)[target].reshape(row_count, top_k, model_width)
    combined = jnp.sum(picked.astype(F32) * gates[:, :, None], axis=1)
    return (after_attn.astype(F32) + combined).astype(BF16)


def append(cache, fresh, length):
    span = cache.shape[0] + fresh.shape[0]
    padded = jnp.concatenate([cache, jnp.zeros_like(fresh)], axis=0)
    kept_rows = jnp.where(
        (jnp.arange(span, dtype=jnp.int32) < length)[:, None], padded, jnp.zeros_like(padded)
    )
    return lax.dynamic_update_slice(kept_rows, fresh, (length, jnp.zeros((), jnp.int32)))


def body(
    hidden_in,
    cache_keys,
    cache_values,
    cache_len,
    attn_gain,
    w_query,
    w_key,
    w_value,
    q_gain,
    k_gain,
    w_out,
    moe_gain,
    expert_ids,
    expert_gates,
    w_gate,
    w_up,
    w_down,
):
    groups, size = lax.axis_size("req"), lax.axis_size("exp")
    z, e = lax.axis_index("req"), lax.axis_index("exp")
    small = groups == 4 and size == 8
    chunks = CHUNKS if small else (ROWS,)
    tokens = hidden_in[0]
    length = cache_len[0]
    hd = q_gain.shape[0]
    heads = w_query.shape[1] // hd
    marks = jnp.stack([length, e, z]).astype(jnp.int32)

    w_qkv = jnp.concatenate([w_query, w_key, w_value], axis=1)
    qkv_pieces = spread(w_qkv, size)
    out_pieces = spread(stage(w_out, [v for b, _, v in qkv_pieces if not b & 1]), size)

    starts = [sum(chunks[:c]) for c in range(len(chunks))]

    def chunked(array):
        blocks = array.reshape((groups, ROWS) + array.shape[1:])
        parts = [
            blocks[:, at : at + rows].reshape((groups * rows,) + array.shape[1:]) for at, rows in zip(starts, chunks)
        ]
        return jnp.concatenate(parts)

    token_at = chunked(jnp.arange(tokens.shape[0], dtype=jnp.int32))
    frequency = THETA ** (-jnp.arange(hd // 2, dtype=F32) * 2.0 / hd)
    angles = (length + token_at).astype(F32)[:, None] * frequency[None, :]
    cosine, sine = jnp.cos(angles), jnp.sin(angles)
    *q, k_new, v_new = project(
        marks,
        chunked(tokens),
        attn_gain[None],
        jnp.concatenate([cosine, cosine], axis=1),
        jnp.concatenate([-sine, sine], axis=1),
        q_gain[None],
        k_gain[None],
        qkv_pieces,
        size,
        heads,
        chunks,
        groups,
    )
    keep = []

    def head_parts(c):
        att, seen = attend(
            marks, q[c], cache_keys[0], cache_values[0], k_new, v_new, starts[c], chunks[c], heads, keep
        )
        parts = out_project(marks, att, out_pieces, size, groups)
        keep[:] = [parts[0]]
        return parts, seen

    if small:
        ids, gates = expert_ids[0], expert_gates[0]
        number = groups * size
        dense = jnp.sum(
            jnp.where(ids[:, :, None] == jnp.arange(number, dtype=jnp.int32), gates[:, :, None], 0.0), axis=1
        )
        gates_to_me = lax.all_to_all(dense.T, ("req", "exp"), split_axis=0, concat_axis=0, tiled=True)
        result_rows, length = by_gathers(
            tokens, gates_to_me, moe_gain, w_gate[0], w_up[0], w_down[0], groups, size, chunks, head_parts
        )
    else:
        resident = lax.dynamic_slice_in_dim(tokens, z * ROWS, ROWS, 0)
        parts = along_sum(head_parts(0)[0], z, groups)
        after, moe_in = add_norm(resident, moe_gain[None], parts)
        result_rows = by_all_to_all(
            expert_ids[0], expert_gates[0], after, moe_in, w_gate[0], w_up[0], w_down[0], groups * size
        )
    keys_out = append(cache_keys[0], k_new, length)
    values_out = append(cache_values[0], v_new, length)
    return (result_rows[None], keys_out[None], values_out[None])


def solution(mesh):
    placed = (
        P("exp", None, None),
        P("exp", None, "req"),
        P("exp", None, "req"),
        P("exp"),
        P(),
        P("exp", "req"),
        P("exp", "req"),
        P("exp", "req"),
        P(),
        P(),
        P(("req", "exp"), None),
        P(),
        P("exp", "req", None),
        P("exp", "req", None),
        P(("req", "exp"), None, None),
        P(("req", "exp"), None, None),
        P(("req", "exp"), None, None),
    )
    return jax.shard_map(
        body,
        mesh=mesh,
        in_specs=placed,
        out_specs=(P("exp", "req", None), P("exp", None, "req"), P("exp", None, "req")),
        check_vma=False,
    )
```

```python
import functools
import math

import jax
import jax.numpy as jnp
from jax import lax
from jax.experimental import pallas as pl
from jax.experimental.pallas import tpu as pltpu
from jax.sharding import PartitionSpec as P

EPS = 1e-06
THETA = 1000000.0
ROWS = 128
ORDER = (0, 2, 1, 3)
HIDE = -1e30
KEYS = 512
TILE = 256
CHUNKS = (64, 64)
WIDE = 1024
REST = 128
MB = 1024 * 1024
F32 = jnp.float32
BF16 = jnp.bfloat16

VMEM = pltpu.VMEM
SMEM = pltpu.SMEM
HBM = pltpu.HBM


def spec(space):
    return pl.BlockSpec(memory_space=space)


def params():
    return pltpu.CompilerParams(vmem_limit_bytes=60 * MB)


def tie_kernel(*refs):
    pass


def tie(values, deps):
    values, deps = list(values), list(deps)
    return pl.pallas_call(
        tie_kernel,
        out_shape=[jax.ShapeDtypeStruct(v.shape, v.dtype) for v in values],
        in_specs=[spec(HBM)] * (len(values) + len(deps)),
        out_specs=[spec(HBM)] * len(values),
        input_output_aliases={i: i for i in range(len(values))},
        compiler_params=params(),
        name="tie",
    )(*values, *deps)


def join_kernel(*refs):
    at = 0
    for ref in refs[:-1]:
        refs[-1][:, at : at + ref.shape[1]] = ref[...]
        at += ref.shape[1]


def join(*parts):
    return pl.pallas_call(
        join_kernel,
        out_shape=jax.ShapeDtypeStruct((parts[0].shape[0], sum(p.shape[1] for p in parts)), parts[0].dtype),
        in_specs=[spec(VMEM)] * len(parts),
        out_specs=spec(VMEM),
        name="join",
    )(*parts)


def swap(value, bit, size):
    return lax.ppermute(value, "exp", [(i, i ^ bit) for i in range(size)])


def shift(value, step, size):
    return lax.ppermute(value, "req", [(i, (i + step) % size) for i in range(size)])


def chip_bits(size):
    bits, bit = [], 2
    while bit < size:
        bits.append(bit)
        bit *= 2
    return bits


def neighbours(value, size):
    return swap(value, 2, size), swap(value, 4, size)


def relays(x, y, size):
    half = x.shape[0] // 2
    return swap(x[:half], 4, size), swap(y[half:], 2, size)


def siblings(pieces, size):
    return pieces + [(b ^ 1, start, swap(v, 1, size)) for b, start, v in pieces]


def listed(value, x, y, first, second):
    return [(0, 0, value), (2, 0, x), (4, 0, y), (6, 0, first), (6, value.shape[0] // 2, second)]


def spread(value, size):
    half = value.shape[0] // 2
    out = []
    for start in (0, half):
        held = {0: value[start : start + half]}
        for bit in chip_bits(size) if start == 0 else chip_bits(size)[::-1]:
            held.update({b ^ bit: swap(v, bit, size) for b, v in list(held.items())})
        out += [(b, start, v) for b, v in held.items()]
    return siblings(out, size)


def add(*terms):
    total = terms[0].astype(F32)
    for term in terms[1:]:
        total = total + term.astype(F32)
    return total.astype(BF16)


def paired(parts, size):
    return {b: (parts[b], swap(parts[b ^ 1], 1, size)) for b in (6, 4, 2, 0)}


def corner(both, size):
    half = both[6][0].shape[0] // 2
    first = add(*(v[:half] for v in both[6]))
    second = add(*(v[half:] for v in both[6]))
    return swap(first, 2, size), swap(second, 4, size)


def beside(both, first, second, size):
    half = first.shape[0]
    x = jnp.concatenate([add(*(v[:half] for v in both[2])), add(*(v[half:] for v in both[2]), second)])
    y = jnp.concatenate([add(*(v[:half] for v in both[4]), first), add(*(v[half:] for v in both[4]))])
    return swap(x, 2, size), swap(y, 4, size)


def along(value, pairs):
    return lax.ppermute(value, "req", pairs)


def along_sum(parts, z, groups):
    if groups != 4:
        return [parts[0]] + [shift(parts[k], k, groups) for k in range(1, groups)]
    up = along(parts[1], [(0, 1), (1, 2), (2, 3)])
    down = along(parts[3], [(1, 0), (2, 1), (3, 2)])
    relayed = along(parts[4], [(0, 1), (3, 2)])
    over = along(add(parts[2], relayed), [(0, 2), (1, 3), (2, 0), (3, 1)])
    return [parts[0], up, down, over]


def along_gather(value, z, groups):
    over = along(value, [(0, 2), (1, 3), (2, 0), (3, 1)])
    up = along(value, [(0, 1), (1, 2), (2, 3)])
    down = along(value, [(1, 0), (2, 1), (3, 2)])
    relayed = along(over, [(1, 0), (2, 3)])
    got = [value, jnp.where(z == 0, relayed, up), over, jnp.where(z == 3, relayed, down)]
    return jnp.concatenate([got[k] for k in ORDER])


def stage_kernel(w_ref, *rest):
    rest[-1][...] = w_ref[...]


def stage(w, extra):
    return pl.pallas_call(
        stage_kernel,
        out_shape=jax.ShapeDtypeStruct(w.shape, w.dtype),
        in_specs=[spec(VMEM)] + [spec(HBM)] * len(extra),
        out_specs=spec(VMEM),
        name="stage",
    )(w, *extra)


def start_loads(e, pieces, at, shard, w_ref, sem):
    copies = []
    for i, (piece, (b, start)) in enumerate(zip(pieces, at)):
        row = pl.multiple_of((e ^ b) * shard + start, 16)
        copy = pltpu.make_async_copy(piece, w_ref.at[pl.ds(row, piece.shape[0])], sem.at[i])
        copy.start()
        copies.append(copy)
    return copies


def project_kernel(marks, x_ref, gain_ref, cos_ref, sin_ref, qg_ref, kg_ref, *rest, at, shard, heads, chunks, groups, extras):
    pieces, rest = rest[: len(at)], rest[len(at) :]
    rest = rest[extras:]
    q_refs, rest = rest[: len(chunks)], rest[len(chunks) :]
    k_ref, v_ref, w_ref, n_ref, sem = rest
    copies = start_loads(marks[1], pieces, at, shard, w_ref, sem)
    x = x_ref[...].astype(F32)
    factor = lax.rsqrt(jnp.mean(x * x, axis=-1, keepdims=True) + EPS)
    n_ref[...] = (x * factor * gain_ref[...]).astype(BF16)
    for copy in copies:
        copy.wait()
    hd = qg_ref.shape[1]
    starts = [sum(chunks[:c]) for c in range(len(chunks))]

    def turned(value, gain):
        factor = lax.rsqrt(jnp.mean(value * value, axis=-1, keepdims=True) + EPS)
        value = value * factor * gain
        return value * cos_ref[...] + pltpu.roll(value, hd // 2, 1) * sin_ref[...]

    scale = hd ** (-0.5) * math.log2(math.e)

    for first in range(0, heads, 4):
        four = jnp.dot(n_ref[...], w_ref[:, first * hd : (first + 4) * hd], preferred_element_type=F32)
        for s in range(4):
            q = (turned(four[:, s * hd : (s + 1) * hd], qg_ref[...]) * scale).astype(BF16)
            for c, rows in enumerate(chunks):
                span = groups * rows
                q_refs[c][(first + s) * span : (first + s + 1) * span] = q[starts[c] * groups :][:span]
    both = jnp.dot(n_ref[...], w_ref[:, heads * hd : (heads + 2) * hd], preferred_element_type=F32)
    k = turned(both[:, :hd], kg_ref[...]).astype(BF16)
    v = both[:, hd:].astype(BF16)
    for c, rows in enumerate(chunks):
        for r in range(groups):
            src = slice(starts[c] * groups + r * rows, starts[c] * groups + (r + 1) * rows)
            dst = slice(r * ROWS + starts[c], r * ROWS + starts[c] + rows)
            k_ref[dst] = k[src]
            v_ref[dst] = v[src]


def project(marks, x, gain, cos, sin, q_gain, k_gain, pieces, size, heads, chunks, groups, extra):
    tokens, width = x.shape
    hd = q_gain.shape[1]
    at = [piece[:2] for piece in pieces]
    pieces = [piece[2] for piece in pieces]
    cols = pieces[0].shape[1]
    return pl.pallas_call(
        functools.partial(project_kernel, at=at, shard=width // size, heads=heads, chunks=chunks, groups=groups, extras=len(extra)),
        out_shape=(
            *(jax.ShapeDtypeStruct((heads * groups * rows, hd), BF16) for rows in chunks),
            jax.ShapeDtypeStruct((tokens, hd), BF16),
            jax.ShapeDtypeStruct((tokens, hd), BF16),
        ),
        in_specs=[spec(SMEM)] + [spec(VMEM)] * 6 + [spec(HBM)] * (len(pieces) + len(extra)),
        out_specs=(spec(VMEM),) * (2 + len(chunks)),
        scratch_shapes=[
            VMEM((width, cols), BF16),
            VMEM((tokens, width), BF16),
            pltpu.SemaphoreType.DMA((len(pieces),)),
        ],
        compiler_params=params(),
        cost_estimate=pl.CostEstimate(flops=2 * tokens * width * cols, bytes_accessed=10 * MB, transcendentals=0),
        name="project",
    )(marks, x, gain, cos, sin, q_gain, k_gain, *pieces, *extra)


def attend_kernel(marks, q_hbm, kc_hbm, vc_hbm, kn_hbm, vn_hbm, *rest, start, rows, heads, at, shard):
    pieces, rest = rest[: len(at)], rest[len(at) :]
    if at:
        rest, (o_ref, w_ref, p_ref, psem) = rest[:-4], rest[-4:]
        *outs, marks_out, qa, ka, va, s0, s1, m0, m1, bias, sem = rest[-15:]
        copies = start_loads(marks[1], pieces, at, shard, w_ref, psem)
    else:
        o_ref, marks_out, qa, ka, va, s0, s1, m0, m1, bias, sem = rest[-11:]
    ctx, hd = kc_hbm.shape
    keys = ctx + kn_hbm.shape[0]
    tokens = qa.shape[0] // heads
    loads = [
        pltpu.make_async_copy(src, dst, sem.at[i])
        for i, (src, dst) in enumerate(
            (
                (q_hbm, qa.at[:, :hd]),
                (kc_hbm, ka.at[:ctx, :hd]),
                (kn_hbm, ka.at[ctx:, :hd]),
                (vc_hbm, va.at[:ctx, :hd]),
                (vn_hbm, va.at[ctx:, :hd]),
            )
        )
    ]
    for load in loads:
        load.start()
    for i in range(3):
        marks_out[i] = marks[i]
    length = marks[0]
    lane = lax.broadcasted_iota(jnp.int32, (1, hd), 1)
    qa[:, hd:] = jnp.broadcast_to(jnp.where(lane == 0, 1.0, 0.0), (heads * tokens, hd)).astype(BF16)
    where = lax.broadcasted_iota(jnp.int32, (keys, hd), 0)
    first = lax.broadcasted_iota(jnp.int32, (keys, hd), 1) == 0
    ka[:, hd:] = jnp.where(first & (where >= length) & (where < ctx), HIDE, 0.0).astype(BF16)
    va[:, hd:] = jnp.ones((keys, hd), BF16)
    tile = bias.shape[0]
    place = lax.broadcasted_iota(jnp.int32, (tile, KEYS), 0) % tokens
    token = (place // rows) * ROWS + start + place % rows
    bias[...] = jnp.where(lax.broadcasted_iota(jnp.int32, (tile, KEYS), 1) <= token, 0.0, HIDE)
    blocks = keys // KEYS
    tiles = heads * tokens // tile
    per = tile // tokens

    for load in loads:
        load.wait()

    def scores(i, buf, j, peak):
        q = qa[pl.ds(pl.multiple_of(i * tile, tile), tile)]
        s = lax.dot_general(q, ka[j * KEYS : (j + 1) * KEYS], (((1,), (1,)), ((), ())), preferred_element_type=F32)
        if j == blocks - 1:
            s = s + bias[...]
        buf[:, j * KEYS : (j + 1) * KEYS] = s
        for c in range(KEYS // hd):
            part = s[:, c * hd : (c + 1) * hd]
            peak = part if peak is None else jnp.maximum(peak, part)
        return peak

    def top(peak):
        return jnp.broadcast_to(jnp.max(peak, axis=1, keepdims=True), (tile, hd))

    def mix(buf, m_ref, j, total):
        m = m_ref[...]
        s = buf[:, j * KEYS : (j + 1) * KEYS]
        p = jnp.concatenate(
            [jnp.exp2(s[:, c * hd : (c + 1) * hd] - m).astype(BF16) for c in range(KEYS // hd)], axis=1
        )
        part = jnp.dot(p, va[j * KEYS : (j + 1) * KEYS], preferred_element_type=F32)
        return part if total is None else total + part

    def finish(i, total):
        out = (total[:, :hd] / total[:, hd:]).astype(BF16)
        for h in range(per):
            o_ref[i * per + h] = out[h * tokens : (h + 1) * tokens]

    bufs, peaks = (s0, s1), (m0, m1)

    def step(i, parity, score, mixing):
        peak = total = None
        for j in range(blocks):
            if score:
                peak = scores(i, bufs[parity], j, peak)
            if mixing:
                total = mix(bufs[1 - parity], peaks[1 - parity], j, total)
        if score:
            peaks[parity][...] = top(peak)
        if mixing:
            finish(i - 1, total)

    step(0, 0, True, False)
    step(1, 1, True, True)

    def two(n, carry):
        step(2 * n, 0, True, True)
        step(2 * n + 1, 1, True, True)
        return carry

    lax.fori_loop(1, tiles // 2, two, 0)
    step(tiles, 0, False, True)
    if at:
        for copy in copies:
            copy.wait()
        att = jnp.concatenate([o_ref[h] for h in range(heads)], axis=1)
        give_out(marks, att, w_ref, p_ref, outs)


def attend(marks, q, kc, vc, kn, vn, start, rows, heads, extra=(), pieces=(), size=0, groups=0):
    hd = q.shape[1]
    tokens = q.shape[0] // heads
    keys = kc.shape[0] + kn.shape[0]
    tile = tokens * max(1, TILE // tokens)
    at = [piece[:2] for piece in pieces]
    pieces = [piece[2] for piece in pieces]
    shape = jax.ShapeDtypeStruct((heads, tokens, hd), BF16)
    scratch = [
        VMEM((heads * tokens, 2 * hd), BF16),
        VMEM((keys, 2 * hd), BF16),
        VMEM((keys, 2 * hd), BF16),
        VMEM((tile, keys), F32),
        VMEM((tile, keys), F32),
        VMEM((tile, hd), F32),
        VMEM((tile, hd), F32),
        VMEM((tile, KEYS), F32),
        pltpu.SemaphoreType.DMA((5,)),
    ]
    shapes = [shape]
    if pieces:
        width = pieces[0].shape[1]
        shapes = [jax.ShapeDtypeStruct((rows, width), BF16)] * (groups + 1)
        scratch += [
            VMEM(shape.shape, BF16),
            VMEM((heads * hd, width), BF16),
            VMEM((groups, rows, width), BF16),
            pltpu.SemaphoreType.DMA((len(pieces),)),
        ]
    return pl.pallas_call(
        functools.partial(
            attend_kernel, start=start, rows=rows, heads=heads, at=at, shard=heads * hd // max(1, size)
        ),
        out_shape=(*shapes, jax.ShapeDtypeStruct((3,), jnp.int32)),
        in_specs=[spec(SMEM)] + [spec(HBM)] * (5 + len(pieces) + len(extra)),
        out_specs=(*(spec(VMEM) for _ in shapes), spec(SMEM)),
        scratch_shapes=scratch,
        compiler_params=params(),
        cost_estimate=pl.CostEstimate(
            flops=8 * heads * tokens * keys * hd, bytes_accessed=4 * MB, transcendentals=heads * tokens * keys
        ),
        name="attend",
    )(marks, q, kc, vc, kn, vn, *pieces, *extra)


def give_out(marks, att, w_ref, o_ref, outs):
    groups, rows, _ = o_ref.shape
    for n in range(0, w_ref.shape[1], WIDE):
        cols = slice(n, n + WIDE)
        part = jnp.dot(att, w_ref[:, cols], preferred_element_type=F32).astype(BF16)
        for r in range(groups):
            o_ref[r, :, cols] = part[r * rows : (r + 1) * rows]
    for k in range(groups):
        outs[k][...] = o_ref[lax.rem(marks[2] + k, groups)]
    outs[groups][...] = o_ref[jnp.where(marks[2] == 0, groups - 1, 0)]


def out_kernel(marks, att_ref, *rest, at, shard):
    pieces, rest = rest[: len(at)], rest[len(at) :]
    outs, (w_ref, o_ref, sem) = rest[:-3], rest[-3:]
    copies = start_loads(marks[1], pieces, at, shard, w_ref, sem)
    att = jnp.concatenate([att_ref[h] for h in range(att_ref.shape[0])], axis=1)
    for copy in copies:
        copy.wait()
    give_out(marks, att, w_ref, o_ref, outs)


def out_project(marks, att, pieces, size, groups):
    heads, tokens, hd = att.shape
    at = [piece[:2] for piece in pieces]
    pieces = [piece[2] for piece in pieces]
    width = pieces[0].shape[1]
    rows = tokens // groups
    return pl.pallas_call(
        functools.partial(out_kernel, at=at, shard=heads * hd // size),
        out_shape=(jax.ShapeDtypeStruct((rows, width), BF16),) * (groups + 1),
        in_specs=[spec(SMEM), spec(VMEM)] + [spec(HBM)] * len(pieces),
        out_specs=(spec(VMEM),) * (groups + 1),
        scratch_shapes=[
            VMEM((heads * hd, width), BF16),
            VMEM((groups, rows, width), BF16),
            pltpu.SemaphoreType.DMA((len(pieces),)),
        ],
        compiler_params=params(),
        cost_estimate=pl.CostEstimate(flops=2 * tokens * heads * hd * width, bytes_accessed=5 * MB, transcendentals=0),
        name="out_project",
    )(marks, att, *pieces)


def norm_kernel(x_ref, gain_ref, *rest, terms):
    parts, (after_ref, moe_ref) = rest[:terms], rest[-2:]
    total = parts[0][...].astype(F32)
    for part in parts[1:]:
        total = total + part[...].astype(F32)
    after = (x_ref[...].astype(F32) + total).astype(BF16)
    after_ref[...] = after
    x = after.astype(F32)
    factor = lax.rsqrt(jnp.mean(x * x, axis=-1, keepdims=True) + EPS)
    moe_ref[...] = (x * factor * gain_ref[...]).astype(BF16)


def add_norm(x, gain, parts, extra=()):
    shape = jax.ShapeDtypeStruct(x.shape, BF16)
    return pl.pallas_call(
        functools.partial(norm_kernel, terms=len(parts)),
        out_shape=(shape, shape),
        in_specs=[spec(VMEM)] * (2 + len(parts)) + [spec(HBM)] * len(extra),
        out_specs=(spec(VMEM),) * 2,
        name="add_norm",
    )(x, gain, *parts, *extra)


def expert_kernel(count_ref, slot_ref, gate_ref, *rest, at, span, extras, size):
    pieces, rest = rest[: len(at)], rest[len(at) :]
    wg_hbm, wu_hbm, wd_hbm = rest[:3]
    outs = rest[3 + extras : 3 + extras + size]
    x_ref, y_ref, wg, wu, wd, xg, hid, sem, wsem, osem = rest[3 + extras + size :]
    width = x_ref.shape[1]
    units, _, tokens = slot_ref.shape
    take = xg.shape[0]
    held = tokens // span
    copies = [
        pltpu.make_async_copy(piece, x_ref.at[b * span + start : b * span + start + piece.shape[0]], sem.at[i])
        for i, (piece, (b, start)) in enumerate(zip(pieces, at))
    ]
    own = [[copy for copy, (b, _) in zip(copies, at) if b // held == unit] for unit in range(units)]
    loads = [
        pltpu.make_async_copy(src, dst, wsem.at[i])
        for i, (src, dst) in enumerate(((wg_hbm, wg), (wu_hbm, wu), (wd_hbm, wd)))
    ]
    for copy in own[0] + loads + sum(own[1:], []):
        copy.start()

    def tile(unit, base, first, take):
        slots = slot_ref[unit]
        slots_t = jnp.transpose(jnp.broadcast_to(slots, (128, tokens)))
        slot = lax.broadcasted_iota(jnp.int32, (take, tokens), 0).astype(F32) + base
        hit = slot == slots
        pick = jnp.where(hit, 1.0, 0.0).astype(BF16)
        gate = jnp.sum(jnp.where(hit, gate_ref[unit], 0.0), axis=1, keepdims=True)
        lane = lax.broadcasted_iota(jnp.int32, (tokens, 128), 1).astype(F32) + base
        put = jnp.concatenate(
            [jnp.where(lane + n == slots_t, 1.0, 0.0).astype(BF16) for n in range(0, take, 128)], axis=1
        )[:, :take]
        if first:
            for copy in own[unit]:
                copy.wait()
        at = slice(unit * tokens, (unit + 1) * tokens)
        for n in range(0, width, WIDE):
            cols = slice(n, n + WIDE)
            xg[:take, cols] = jnp.dot(pick, x_ref[at, cols], preferred_element_type=F32).astype(BF16)
        if first and unit == 0:
            loads[0].wait()
            loads[1].wait()
        g = jnp.dot(xg[:take], wg[...], preferred_element_type=F32)
        u = jnp.dot(xg[:take], wu[...], preferred_element_type=F32)
        hid[:take] = (g / (1.0 + jnp.exp(-g)) * u).astype(BF16)
        if first and unit == 0:
            loads[2].wait()
        for n in range(0, width, WIDE):
            cols = slice(n, n + WIDE)
            o = jnp.dot(hid[:take], wd[:, cols], preferred_element_type=F32).astype(BF16)
            o = (o.astype(F32) * gate).astype(BF16)
            back = jnp.dot(put, o, preferred_element_type=F32).astype(BF16)
            y_ref[at, cols] = back if first else y_ref[at, cols] + back

    sends = []
    for unit in range(units):
        tile(unit, 0.0, True, take)

        def more(i, carry):
            tile(unit, (take + i * REST).astype(F32), False, REST)
            return carry

        lax.fori_loop(0, lax.div(jnp.maximum(count_ref[unit] - take, 0) + (REST - 1), REST), more, 0)
        for b in range(unit * held, (unit + 1) * held):
            send = pltpu.make_async_copy(y_ref.at[b * span : (b + 1) * span], outs[b], osem.at[b])
            send.start()
            sends.append(send)
    for send in sends:
        send.wait()


def experts(count, slots, gate, pieces, wg, wu, wd, extra, size):
    at = [piece[:2] for piece in pieces]
    pieces = [piece[2] for piece in pieces]
    span, width = pieces[0].shape
    tokens = size * span
    take = slots.shape[2] * 6 // 16
    ratio = 2 * slots.shape[0]
    n = len(pieces)
    ff = wg.shape[1]
    return pl.pallas_call(
        functools.partial(expert_kernel, at=at, span=span, extras=len(extra), size=size),
        out_shape=(jax.ShapeDtypeStruct((span, width), BF16),) * size,
        in_specs=[spec(SMEM)] + [spec(VMEM)] * 2 + [spec(HBM)] * (n + 3 + len(extra)),
        out_specs=(spec(HBM),) * size,
        scratch_shapes=[
            VMEM((tokens, width), BF16),
            VMEM((tokens, width), BF16),
            VMEM(wg.shape, BF16),
            VMEM(wu.shape, BF16),
            VMEM(wd.shape, BF16),
            VMEM((take, width), BF16),
            VMEM((take, ff), BF16),
            pltpu.SemaphoreType.DMA((n,)),
            pltpu.SemaphoreType.DMA((3,)),
            pltpu.SemaphoreType.DMA((size,)),
        ],
        compiler_params=params(),
        cost_estimate=pl.CostEstimate(
            flops=ratio * (6 * take * width * ff + 4 * take * tokens * width), bytes_accessed=18 * MB, transcendentals=0
        ),
        name="experts",
    )(count, slots, gate, *pieces, wg, wu, wd, *extra)


def route(mine, size, groups):
    span = groups * mine.shape[1]
    units = 1
    while size * span // units > 1024:
        units *= 2
    mine = mine.reshape(units, -1)
    at = jnp.arange(mine.shape[1], dtype=jnp.int32)
    routed = mine > 0
    before = jnp.dot(routed.astype(BF16), (at[:, None] < at[None, :]).astype(BF16), preferred_element_type=F32)
    slots = jnp.where(routed, before, -1.0)
    return mine[:, None], slots[:, None], jnp.sum(routed.astype(jnp.int32), axis=1)


def by_gathers(tokens, gates_to_me, moe_gain, w_gate, w_up, w_down, groups, size, chunks, head_parts, late):
    z = lax.axis_index("req")
    resident = lax.dynamic_slice_in_dim(tokens, z * ROWS, ROWS, 0)
    starts = [sum(chunks[:c]) for c in range(len(chunks))]
    number = len(chunks)
    kept, stacks = [], []

    def settle(c, parts, extra=()):
        rows = resident[starts[c] : starts[c] + chunks[c]]
        after, moe_in = add_norm(rows, moe_gain[None], along_sum(parts, z, groups), extra)
        kept.append(after)
        stacks.append(along_gather(moe_in, z, groups))
        return moe_in

    for c in range(number):
        extra = [] if c == 0 else [parts[0]]
        if c >= 2:
            settle(c - 2, waiting)
            extra += [stacks[c - 2]]
        if c >= 1:
            waiting = parts
        parts, marks = head_parts(c, extra)
        if c == 0:
            near_e = jnp.arange(size, dtype=jnp.int32)[:, None] ^ marks[1]
            far = (marks[2] - jnp.array(ORDER, jnp.int32)[None]) % groups
            near_first = gates_to_me[(far * size + near_e).reshape(-1)]
    settle(number - 2, waiting, [parts[0]])
    settle(number - 1, parts)

    routed_to_me = [route(near_first[:, starts[c] : starts[c] + rows], size, groups) for c, rows in enumerate(chunks)]
    appended = late([kept[0]] + [v for group in routed_to_me for v in group])
    near, results, both, out = [], [], [None] * number, [None] * number
    sides, corners = [], []
    near.append(neighbours(stacks[0], size))

    def finish(c):
        rows = chunks[c]
        terms = both[c][0] + sides[c]
        cut = {k: add(*(term[i * rows : (i + 1) * rows] for term in terms)) for i, k in enumerate(ORDER)}
        parts = [cut[0]] + [shift(cut[k], -k, groups) for k in (2, 1, 3)]
        return add(kept[c], *parts)

    for c, rows in enumerate(chunks):
        mine, slots, count = routed_to_me[c]
        x, y = near[c]
        pieces = siblings(listed(stacks[c], x, y, *relays(x, y, size)), size)
        extra = []
        if c == 0:
            extra += list(appended)
        else:
            extra += list(corners[c - 1])
        if c + 1 < number:
            extra += [stacks[c + 1]]
            near.append(neighbours(stacks[c + 1], size))
        made = experts(count, slots, mine, pieces, w_gate, w_up, w_down, extra, size)
        deps = []
        if c + 1 < number:
            deps += list(near[c + 1])
        if c > 0:
            sides.append(beside(both[c - 1], *corners[c - 1], size))
            deps += list(sides[c - 1])
        made = tie(made, deps) if deps else made
        both[c] = paired(made, size)
        corners.append(corner(both[c], size))
        if c > 0:
            results.append(finish(c - 1))
    sides.append(beside(both[-1], *corners[-1], size))
    results.append(finish(number - 1))
    return jnp.concatenate(results), appended


def by_all_to_all(routes, gates, after_attn, moe_in, w_gate, w_up, w_down, experts_n):
    row_count, model_width = moe_in.shape
    top_k = routes.shape[1]
    capacity = 3 * top_k * row_count // (2 * experts_n)
    flat_ids = routes.reshape(-1)
    onehot = (flat_ids[:, None] == jnp.arange(experts_n, dtype=jnp.int32)[None, :]).astype(jnp.int32)
    slots = jnp.sum((jnp.cumsum(onehot, axis=0) - 1) * onehot, axis=1)
    target = flat_ids * capacity + slots
    sources = jnp.arange(row_count * top_k, dtype=jnp.int32) // top_k
    outgoing = jnp.zeros((experts_n * capacity, model_width), BF16).at[target].set(moe_in[sources])
    outgoing = outgoing.reshape(experts_n, capacity, model_width)
    block_in = lax.all_to_all(outgoing, ("req", "exp"), split_axis=0, concat_axis=0, tiled=True)
    flat_rows = block_in.reshape(-1, model_width)
    gate_proj = jnp.dot(flat_rows, w_gate, preferred_element_type=F32)
    up_proj = jnp.dot(flat_rows, w_up, preferred_element_type=F32)
    activated = (jax.nn.silu(gate_proj) * up_proj).astype(BF16)
    produced = jnp.dot(activated, w_down, preferred_element_type=F32).astype(BF16)
    returned = lax.all_to_all(
        produced.reshape(block_in.shape), ("req", "exp"), split_axis=0, concat_axis=0, tiled=True
    )
    picked = returned.reshape(experts_n * capacity, model_width)[target].reshape(row_count, top_k, model_width)
    combined = jnp.sum(picked.astype(F32) * gates[:, :, None], axis=1)
    return (after_attn.astype(F32) + combined).astype(BF16)


def append_kernel(marks, kc_ref, vc_ref, kn_ref, vn_ref, *rest):
    k_out, v_out, k_all, v_all, sem = rest[-5:]
    ctx, hd = kc_ref.shape
    fresh = kn_ref.shape[0]
    length = marks[0]
    base = pl.multiple_of(lax.div(length, 16) * 16, 16)
    window = fresh + 16
    kept = lax.broadcasted_iota(jnp.int32, (ctx, hd), 0) < length
    row = lax.broadcasted_iota(jnp.int32, (window, fresh), 0) - (length - base)
    move = jnp.where(row == lax.broadcasted_iota(jnp.int32, (window, fresh), 1), 1.0, 0.0).astype(BF16)
    old = lax.broadcasted_iota(jnp.int32, (window, hd), 0) < length - base
    copies = []
    sides = ((kc_ref, kn_ref, k_all, k_out), (vc_ref, vn_ref, v_all, v_out))
    for i, (cache, new, whole, out) in enumerate(sides):
        whole[:ctx] = jnp.where(kept, cache[...].astype(F32), 0.0).astype(BF16)
        whole[ctx:] = jnp.zeros((whole.shape[0] - ctx, hd), BF16)
        added = jnp.dot(move, new[...], preferred_element_type=F32)
        at = pl.ds(base, window)
        whole[at] = jnp.where(old, whole[at].astype(F32), added).astype(BF16)
        copy = pltpu.make_async_copy(whole.at[: ctx + fresh], out, sem.at[i])
        copy.start()
        copies.append(copy)
    for copy in copies:
        copy.wait()


def append(marks, kc, vc, kn, vn, extra=()):
    rows, hd = kc.shape[0] + kn.shape[0], kc.shape[1]
    shape = jax.ShapeDtypeStruct((rows, hd), BF16)
    return pl.pallas_call(
        append_kernel,
        out_shape=(shape, shape),
        in_specs=[spec(SMEM)] + [spec(VMEM)] * 4 + [spec(HBM)] * len(extra),
        out_specs=(spec(HBM),) * 2,
        scratch_shapes=[VMEM((rows + 16, hd), BF16), VMEM((rows + 16, hd), BF16), pltpu.SemaphoreType.DMA((2,))],
        compiler_params=params(),
        cost_estimate=pl.CostEstimate(flops=0, bytes_accessed=5 * MB, transcendentals=0),
        name="append",
    )(marks, kc, vc, kn, vn, *extra)


def body(
    hidden_in,
    cache_keys,
    cache_values,
    cache_len,
    attn_gain,
    w_query,
    w_key,
    w_value,
    q_gain,
    k_gain,
    w_out,
    moe_gain,
    expert_ids,
    expert_gates,
    w_gate,
    w_up,
    w_down,
):
    groups, size = lax.axis_size("req"), lax.axis_size("exp")
    z, e = lax.axis_index("req"), lax.axis_index("exp")
    small = groups == 4 and size == 8
    chunks = CHUNKS if small else (ROWS,)
    tokens = hidden_in[0]
    length = cache_len[0]
    hd = q_gain.shape[0]
    heads = w_query.shape[1] // hd
    marks = jnp.stack([length, e, z]).astype(jnp.int32)

    w_qkv = join(w_query, w_key, w_value)
    if small:
        x, y = neighbours(w_qkv, size)
        first, second = relays(x, y, size)
        qkv_pieces = siblings(listed(w_qkv, x, y, first, second), size)
        w_out = stage(w_out, [x, y])
        out_x, out_y = neighbours(w_out, size)
    else:
        qkv_pieces = spread(w_qkv, size)
        out_pieces = spread(w_out, size)

    if small:
        ids, gates = expert_ids[0], expert_gates[0]
        number = groups * size
        dense = jnp.sum(
            jnp.where(ids[:, :, None] == jnp.arange(number, dtype=jnp.int32), gates[:, :, None], 0.0), axis=1
        )
        gates_to_me = lax.all_to_all(dense.T, ("req", "exp"), split_axis=0, concat_axis=0, tiled=True)

    starts = [sum(chunks[:c]) for c in range(len(chunks))]

    def chunked(array):
        blocks = array.reshape((groups, ROWS) + array.shape[1:])
        parts = [
            blocks[:, at : at + rows].reshape((groups * rows,) + array.shape[1:]) for at, rows in zip(starts, chunks)
        ]
        return jnp.concatenate(parts)

    token_at = chunked(jnp.arange(tokens.shape[0], dtype=jnp.int32))
    frequency = THETA ** (-jnp.arange(hd // 2, dtype=F32) * 2.0 / hd)
    angles = (length + token_at).astype(F32)[:, None] * frequency[None, :]
    cosine, sine = jnp.cos(angles), jnp.sin(angles)
    *q, k_new, v_new = project(
        marks,
        chunked(tokens),
        attn_gain[None],
        jnp.concatenate([cosine, cosine], axis=1),
        jnp.concatenate([-sine, sine], axis=1),
        q_gain[None],
        k_gain[None],
        qkv_pieces,
        size,
        heads,
        chunks,
        groups,
        [gates_to_me] if small else [],
    )
    pieces = []

    def head_parts(c, extra):
        args = marks, q[c], cache_keys[0], cache_values[0], k_new, v_new, starts[c], chunks[c], heads, extra
        if c == 0:
            att, seen = attend(*args)
            pieces[:] = out_pieces(att) if small else out_pieces
            return out_project(marks, att, pieces, size, groups), seen
        *parts, seen = attend(*args, pieces, size, groups)
        return parts, seen

    if small:
        out_x, out_y = tie([out_x, out_y], [k_new])
        out_first, out_second = relays(out_x, out_y, size)

        def out_pieces(att):
            first, second = tie([out_first, out_second], [att])
            return siblings(listed(w_out, out_x, out_y, first, second), size)

    def late(extra):
        return append(marks, cache_keys[0], cache_values[0], k_new, v_new, extra)

    if small:
        result_rows, (keys_out, values_out) = by_gathers(
            tokens, gates_to_me, moe_gain, w_gate[0], w_up[0], w_down[0], groups, size, chunks, head_parts, late
        )
    else:
        resident = lax.dynamic_slice_in_dim(tokens, z * ROWS, ROWS, 0)
        parts = along_sum(head_parts(0, [])[0], z, groups)
        after, moe_in = add_norm(resident, moe_gain[None], parts)
        result_rows = by_all_to_all(
            expert_ids[0], expert_gates[0], after, moe_in, w_gate[0], w_up[0], w_down[0], groups * size
        )
        keys_out, values_out = late([after])
    return (result_rows[None], keys_out[None], values_out[None])


def solution(mesh):
    placed = (
        P("exp", None, None),
        P("exp", None, "req"),
        P("exp", None, "req"),
        P("exp"),
        P(),
        P("exp", "req"),
        P("exp", "req"),
        P("exp", "req"),
        P(),
        P(),
        P(("req", "exp"), None),
        P(),
        P("exp", "req", None),
        P("exp", "req", None),
        P(("req", "exp"), None, None),
        P(("req", "exp"), None, None),
        P(("req", "exp"), None, None),
    )
    return jax.shard_map(
        body,
        mesh=mesh,
        in_specs=placed,
        out_specs=(P("exp", "req", None), P("exp", None, "req"), P("exp", None, "req")),
        check_vma=False,
    )
```

```python
import functools
import math

import jax
import jax.numpy as jnp
from jax import lax
from jax.experimental import pallas as pl
from jax.experimental.pallas import tpu as pltpu
from jax.sharding import PartitionSpec as P

EPS = 1e-06
THETA = 1000000.0
ROWS = 128
ORDER = (0, 2, 1, 3)
HIDE = -1e30
KEYS = 512
TILE = 256
CHUNKS = (64, 64)
WIDE = 1024
REST = 128
MB = 1024 * 1024
F32 = jnp.float32
BF16 = jnp.bfloat16

VMEM = pltpu.VMEM
SMEM = pltpu.SMEM
HBM = pltpu.HBM


def spec(space):
    return pl.BlockSpec(memory_space=space)


def params():
    return pltpu.CompilerParams(vmem_limit_bytes=60 * MB)


def tie_kernel(*refs):
    pass


def tie(values, deps):
    values, deps = list(values), list(deps)
    return pl.pallas_call(
        tie_kernel,
        out_shape=[jax.ShapeDtypeStruct(v.shape, v.dtype) for v in values],
        in_specs=[spec(HBM)] * (len(values) + len(deps)),
        out_specs=[spec(HBM)] * len(values),
        input_output_aliases={i: i for i in range(len(values))},
        compiler_params=params(),
        name="tie",
    )(*values, *deps)


def join_kernel(*refs):
    at = 0
    for ref in refs[:-1]:
        refs[-1][:, at : at + ref.shape[1]] = ref[...]
        at += ref.shape[1]


def join(*parts):
    return pl.pallas_call(
        join_kernel,
        out_shape=jax.ShapeDtypeStruct((parts[0].shape[0], sum(p.shape[1] for p in parts)), parts[0].dtype),
        in_specs=[spec(VMEM)] * len(parts),
        out_specs=spec(VMEM),
        name="join",
    )(*parts)


def swap(value, bit, size):
    return lax.ppermute(value, "exp", [(i, i ^ bit) for i in range(size)])


def shift(value, step, size):
    return lax.ppermute(value, "req", [(i, (i + step) % size) for i in range(size)])


def chip_bits(size):
    bits, bit = [], 2
    while bit < size:
        bits.append(bit)
        bit *= 2
    return bits


def neighbours(value, size):
    return swap(value, 2, size), swap(value, 4, size)


def relays(x, y, size):
    half = x.shape[0] // 2
    return swap(x[:half], 4, size), swap(y[half:], 2, size)


def siblings(pieces, size):
    return pieces + [(b ^ 1, start, swap(v, 1, size)) for b, start, v in pieces]


def listed(value, x, y, first, second):
    return [(0, 0, value), (2, 0, x), (4, 0, y), (6, 0, first), (6, value.shape[0] // 2, second)]


def spread(value, size):
    half = value.shape[0] // 2
    out = []
    for start in (0, half):
        held = {0: value[start : start + half]}
        for bit in chip_bits(size) if start == 0 else chip_bits(size)[::-1]:
            held.update({b ^ bit: swap(v, bit, size) for b, v in list(held.items())})
        out += [(b, start, v) for b, v in held.items()]
    return siblings(out, size)


def add(*terms):
    total = terms[0].astype(F32)
    for term in terms[1:]:
        total = total + term.astype(F32)
    return total.astype(BF16)


def paired(parts, size):
    return {b: (parts[b], swap(parts[b ^ 1], 1, size)) for b in (6, 4, 2, 0)}


def corner(both, size):
    half = both[6][0].shape[0] // 2
    first = add(*(v[:half] for v in both[6]))
    second = add(*(v[half:] for v in both[6]))
    return swap(first, 2, size), swap(second, 4, size)


def beside(both, first, second, size):
    half = first.shape[0]
    x = jnp.concatenate([add(*(v[:half] for v in both[2])), add(*(v[half:] for v in both[2]), second)])
    y = jnp.concatenate([add(*(v[:half] for v in both[4]), first), add(*(v[half:] for v in both[4]))])
    return swap(x, 2, size), swap(y, 4, size)


def along(value, pairs):
    return lax.ppermute(value, "req", pairs)


def along_sum(parts, z, groups):
    if groups != 4:
        return [parts[0]] + [shift(parts[k], k, groups) for k in range(1, groups)]
    up = along(parts[1], [(0, 1), (1, 2), (2, 3)])
    down = along(parts[3], [(1, 0), (2, 1), (3, 2)])
    relayed = along(parts[4], [(0, 1), (3, 2)])
    over = along(add(parts[2], relayed), [(0, 2), (1, 3), (2, 0), (3, 1)])
    return [parts[0], up, down, over]


def along_gather(value, z, groups):
    over = along(value, [(0, 2), (1, 3), (2, 0), (3, 1)])
    up = along(value, [(0, 1), (1, 2), (2, 3)])
    down = along(value, [(1, 0), (2, 1), (3, 2)])
    relayed = along(over, [(1, 0), (2, 3)])
    got = [value, jnp.where(z == 0, relayed, up), over, jnp.where(z == 3, relayed, down)]
    return jnp.concatenate([got[k] for k in ORDER])


def stage_kernel(w_ref, *rest):
    rest[-1][...] = w_ref[...]


def stage(w, extra):
    return pl.pallas_call(
        stage_kernel,
        out_shape=jax.ShapeDtypeStruct(w.shape, w.dtype),
        in_specs=[spec(VMEM)] + [spec(HBM)] * len(extra),
        out_specs=spec(VMEM),
        name="stage",
    )(w, *extra)


def start_loads(e, pieces, at, shard, w_ref, sem):
    copies = []
    for i, (piece, (b, start)) in enumerate(zip(pieces, at)):
        row = pl.multiple_of((e ^ b) * shard + start, 16)
        copy = pltpu.make_async_copy(piece, w_ref.at[pl.ds(row, piece.shape[0])], sem.at[i])
        copy.start()
        copies.append(copy)
    return copies


def project_kernel(marks, x_ref, gain_ref, cos_ref, sin_ref, qg_ref, kg_ref, *rest, at, shard, heads, chunks, groups, extras):
    pieces, rest = rest[: len(at)], rest[len(at) :]
    rest = rest[extras:]
    q_refs, rest = rest[: len(chunks)], rest[len(chunks) :]
    k_ref, v_ref, w_ref, n_ref, sem = rest
    copies = start_loads(marks[1], pieces, at, shard, w_ref, sem)
    x = x_ref[...].astype(F32)
    factor = lax.rsqrt(jnp.mean(x * x, axis=-1, keepdims=True) + EPS)
    n_ref[...] = (x * factor * gain_ref[...]).astype(BF16)
    for copy in copies:
        copy.wait()
    hd = qg_ref.shape[1]
    starts = [sum(chunks[:c]) for c in range(len(chunks))]

    def turned(value, gain):
        factor = lax.rsqrt(jnp.mean(value * value, axis=-1, keepdims=True) + EPS)
        value = value * factor * gain
        return value * cos_ref[...] + pltpu.roll(value, hd // 2, 1) * sin_ref[...]

    scale = hd ** (-0.5) * math.log2(math.e)

    for first in range(0, heads, 4):
        four = jnp.dot(n_ref[...], w_ref[:, first * hd : (first + 4) * hd], preferred_element_type=F32)
        for s in range(4):
            q = (turned(four[:, s * hd : (s + 1) * hd], qg_ref[...]) * scale).astype(BF16)
            for c, rows in enumerate(chunks):
                span = groups * rows
                q_refs[c][(first + s) * span : (first + s + 1) * span] = q[starts[c] * groups :][:span]
    both = jnp.dot(n_ref[...], w_ref[:, heads * hd : (heads + 2) * hd], preferred_element_type=F32)
    k = turned(both[:, :hd], kg_ref[...]).astype(BF16)
    v = both[:, hd:].astype(BF16)
    for c, rows in enumerate(chunks):
        for r in range(groups):
            src = slice(starts[c] * groups + r * rows, starts[c] * groups + (r + 1) * rows)
            dst = slice(r * ROWS + starts[c], r * ROWS + starts[c] + rows)
            k_ref[dst] = k[src]
            v_ref[dst] = v[src]


def project(marks, x, gain, cos, sin, q_gain, k_gain, pieces, size, heads, chunks, groups, extra):
    tokens, width = x.shape
    hd = q_gain.shape[1]
    at = [piece[:2] for piece in pieces]
    pieces = [piece[2] for piece in pieces]
    cols = pieces[0].shape[1]
    return pl.pallas_call(
        functools.partial(project_kernel, at=at, shard=width // size, heads=heads, chunks=chunks, groups=groups, extras=len(extra)),
        out_shape=(
            *(jax.ShapeDtypeStruct((heads * groups * rows, hd), BF16) for rows in chunks),
            jax.ShapeDtypeStruct((tokens, hd), BF16),
            jax.ShapeDtypeStruct((tokens, hd), BF16),
        ),
        in_specs=[spec(SMEM)] + [spec(VMEM)] * 6 + [spec(HBM)] * (len(pieces) + len(extra)),
        out_specs=(spec(VMEM),) * (2 + len(chunks)),
        scratch_shapes=[
            VMEM((width, cols), BF16),
            VMEM((tokens, width), BF16),
            pltpu.SemaphoreType.DMA((len(pieces),)),
        ],
        compiler_params=params(),
        cost_estimate=pl.CostEstimate(flops=2 * tokens * width * cols, bytes_accessed=10 * MB, transcendentals=0),
        name="project",
    )(marks, x, gain, cos, sin, q_gain, k_gain, *pieces, *extra)


def attend_kernel(marks, q_hbm, kc_hbm, vc_hbm, kn_hbm, vn_hbm, *rest, start, rows, heads, at, shard):
    pieces, rest = rest[: len(at)], rest[len(at) :]
    if at:
        rest, (o_ref, w_ref, p_ref, psem) = rest[:-4], rest[-4:]
        *outs, marks_out, qa, ka, va, s0, s1, m0, m1, bias, sem = rest[-15:]
        copies = start_loads(marks[1], pieces, at, shard, w_ref, psem)
    else:
        o_ref, marks_out, qa, ka, va, s0, s1, m0, m1, bias, sem = rest[-11:]
    ctx, hd = kc_hbm.shape
    keys = ctx + kn_hbm.shape[0]
    tokens = qa.shape[0] // heads
    loads = [
        pltpu.make_async_copy(src, dst, sem.at[i])
        for i, (src, dst) in enumerate(
            (
                (q_hbm, qa.at[:, :hd]),
                (kc_hbm, ka.at[:ctx, :hd]),
                (kn_hbm, ka.at[ctx:, :hd]),
                (vc_hbm, va.at[:ctx, :hd]),
                (vn_hbm, va.at[ctx:, :hd]),
            )
        )
    ]
    for load in loads:
        load.start()
    for i in range(3):
        marks_out[i] = marks[i]
    length = marks[0]
    lane = lax.broadcasted_iota(jnp.int32, (1, hd), 1)
    qa[:, hd:] = jnp.broadcast_to(jnp.where(lane == 0, 1.0, 0.0), (heads * tokens, hd)).astype(BF16)
    where = lax.broadcasted_iota(jnp.int32, (keys, hd), 0)
    first = lax.broadcasted_iota(jnp.int32, (keys, hd), 1) == 0
    ka[:, hd:] = jnp.where(first & (where >= length) & (where < ctx), HIDE, 0.0).astype(BF16)
    va[:, hd:] = jnp.ones((keys, hd), BF16)
    tile = bias.shape[0]
    place = lax.broadcasted_iota(jnp.int32, (tile, KEYS), 0) % tokens
    token = (place // rows) * ROWS + start + place % rows
    bias[...] = jnp.where(lax.broadcasted_iota(jnp.int32, (tile, KEYS), 1) <= token, 0.0, HIDE)
    blocks = keys // KEYS
    tiles = heads * tokens // tile
    per = tile // tokens

    for load in loads:
        load.wait()

    def scores(i, buf, j, peak):
        q = qa[pl.ds(pl.multiple_of(i * tile, tile), tile)]
        s = lax.dot_general(q, ka[j * KEYS : (j + 1) * KEYS], (((1,), (1,)), ((), ())), preferred_element_type=F32)
        if j == blocks - 1:
            s = s + bias[...]
        buf[:, j * KEYS : (j + 1) * KEYS] = s
        for c in range(KEYS // hd):
            part = s[:, c * hd : (c + 1) * hd]
            peak = part if peak is None else jnp.maximum(peak, part)
        return peak

    def top(peak):
        return jnp.broadcast_to(jnp.max(peak, axis=1, keepdims=True), (tile, hd))

    def mix(buf, m_ref, j, total):
        m = m_ref[...]
        s = buf[:, j * KEYS : (j + 1) * KEYS]
        p = jnp.concatenate(
            [jnp.exp2(s[:, c * hd : (c + 1) * hd] - m).astype(BF16) for c in range(KEYS // hd)], axis=1
        )
        part = jnp.dot(p, va[j * KEYS : (j + 1) * KEYS], preferred_element_type=F32)
        return part if total is None else total + part

    def finish(i, total):
        out = (total[:, :hd] / total[:, hd:]).astype(BF16)
        for h in range(per):
            o_ref[i * per + h] = out[h * tokens : (h + 1) * tokens]

    bufs, peaks = (s0, s1), (m0, m1)

    def step(i, parity, score, mixing):
        peak = total = None
        for j in range(blocks):
            if score:
                peak = scores(i, bufs[parity], j, peak)
            if mixing:
                total = mix(bufs[1 - parity], peaks[1 - parity], j, total)
        if score:
            peaks[parity][...] = top(peak)
        if mixing:
            finish(i - 1, total)

    step(0, 0, True, False)
    step(1, 1, True, True)

    def two(n, carry):
        step(2 * n, 0, True, True)
        step(2 * n + 1, 1, True, True)
        return carry

    lax.fori_loop(1, tiles // 2, two, 0)
    step(tiles, 0, False, True)
    if at:
        for copy in copies:
            copy.wait()
        att = jnp.concatenate([o_ref[h] for h in range(heads)], axis=1)
        give_out(marks, att, w_ref, p_ref, outs)


def attend(marks, q, kc, vc, kn, vn, start, rows, heads, extra=(), pieces=(), size=0, groups=0):
    hd = q.shape[1]
    tokens = q.shape[0] // heads
    keys = kc.shape[0] + kn.shape[0]
    tile = tokens * max(1, TILE // tokens)
    at = [piece[:2] for piece in pieces]
    pieces = [piece[2] for piece in pieces]
    shape = jax.ShapeDtypeStruct((heads, tokens, hd), BF16)
    scratch = [
        VMEM((heads * tokens, 2 * hd), BF16),
        VMEM((keys, 2 * hd), BF16),
        VMEM((keys, 2 * hd), BF16),
        VMEM((tile, keys), F32),
        VMEM((tile, keys), F32),
        VMEM((tile, hd), F32),
        VMEM((tile, hd), F32),
        VMEM((tile, KEYS), F32),
        pltpu.SemaphoreType.DMA((5,)),
    ]
    shapes = [shape]
    if pieces:
        width = pieces[0].shape[1]
        shapes = [jax.ShapeDtypeStruct((rows, width), BF16)] * (groups + 1)
        scratch += [
            VMEM(shape.shape, BF16),
            VMEM((heads * hd, width), BF16),
            VMEM((groups, rows, width), BF16),
            pltpu.SemaphoreType.DMA((len(pieces),)),
        ]
    return pl.pallas_call(
        functools.partial(
            attend_kernel, start=start, rows=rows, heads=heads, at=at, shard=heads * hd // max(1, size)
        ),
        out_shape=(*shapes, jax.ShapeDtypeStruct((3,), jnp.int32)),
        in_specs=[spec(SMEM)] + [spec(HBM)] * (5 + len(pieces) + len(extra)),
        out_specs=(*(spec(VMEM) for _ in shapes), spec(SMEM)),
        scratch_shapes=scratch,
        compiler_params=params(),
        cost_estimate=pl.CostEstimate(
            flops=8 * heads * tokens * keys * hd, bytes_accessed=4 * MB, transcendentals=heads * tokens * keys
        ),
        name="attend",
    )(marks, q, kc, vc, kn, vn, *pieces, *extra)


def give_out(marks, att, w_ref, o_ref, outs):
    groups, rows, _ = o_ref.shape
    for n in range(0, w_ref.shape[1], WIDE):
        cols = slice(n, n + WIDE)
        part = jnp.dot(att, w_ref[:, cols], preferred_element_type=F32).astype(BF16)
        for r in range(groups):
            o_ref[r, :, cols] = part[r * rows : (r + 1) * rows]
    for k in range(groups):
        outs[k][...] = o_ref[lax.rem(marks[2] + k, groups)]
    outs[groups][...] = o_ref[jnp.where(marks[2] == 0, groups - 1, 0)]


def out_kernel(marks, att_ref, *rest, at, shard):
    pieces, rest = rest[: len(at)], rest[len(at) :]
    outs, (w_ref, o_ref, sem) = rest[:-3], rest[-3:]
    copies = start_loads(marks[1], pieces, at, shard, w_ref, sem)
    att = jnp.concatenate([att_ref[h] for h in range(att_ref.shape[0])], axis=1)
    for copy in copies:
        copy.wait()
    give_out(marks, att, w_ref, o_ref, outs)


def out_project(marks, att, pieces, size, groups):
    heads, tokens, hd = att.shape
    at = [piece[:2] for piece in pieces]
    pieces = [piece[2] for piece in pieces]
    width = pieces[0].shape[1]
    rows = tokens // groups
    return pl.pallas_call(
        functools.partial(out_kernel, at=at, shard=heads * hd // size),
        out_shape=(jax.ShapeDtypeStruct((rows, width), BF16),) * (groups + 1),
        in_specs=[spec(SMEM), spec(VMEM)] + [spec(HBM)] * len(pieces),
        out_specs=(spec(VMEM),) * (groups + 1),
        scratch_shapes=[
            VMEM((heads * hd, width), BF16),
            VMEM((groups, rows, width), BF16),
            pltpu.SemaphoreType.DMA((len(pieces),)),
        ],
        compiler_params=params(),
        cost_estimate=pl.CostEstimate(flops=2 * tokens * heads * hd * width, bytes_accessed=5 * MB, transcendentals=0),
        name="out_project",
    )(marks, att, *pieces)


def norm_kernel(x_ref, gain_ref, *rest, terms):
    parts, (after_ref, moe_ref) = rest[:terms], rest[-2:]
    total = parts[0][...].astype(F32)
    for part in parts[1:]:
        total = total + part[...].astype(F32)
    after = (x_ref[...].astype(F32) + total).astype(BF16)
    after_ref[...] = after
    x = after.astype(F32)
    factor = lax.rsqrt(jnp.mean(x * x, axis=-1, keepdims=True) + EPS)
    moe_ref[...] = (x * factor * gain_ref[...]).astype(BF16)


def add_norm(x, gain, parts, extra=()):
    shape = jax.ShapeDtypeStruct(x.shape, BF16)
    return pl.pallas_call(
        functools.partial(norm_kernel, terms=len(parts)),
        out_shape=(shape, shape),
        in_specs=[spec(VMEM)] * (2 + len(parts)) + [spec(HBM)] * len(extra),
        out_specs=(spec(VMEM),) * 2,
        name="add_norm",
    )(x, gain, *parts, *extra)


def expert_kernel(count_ref, slot_ref, gate_ref, *rest, at, span, extras, size):
    pieces, rest = rest[: len(at)], rest[len(at) :]
    wg_hbm, wu_hbm, wd_hbm = rest[:3]
    outs = rest[3 + extras : 3 + extras + size]
    x_ref, y_ref, wg, wu, wd, xg, hid, sem, wsem, osem = rest[3 + extras + size :]
    width = x_ref.shape[1]
    units, _, tokens = slot_ref.shape
    take = xg.shape[0]
    held = tokens // span
    copies = [
        pltpu.make_async_copy(piece, x_ref.at[b * span + start : b * span + start + piece.shape[0]], sem.at[i])
        for i, (piece, (b, start)) in enumerate(zip(pieces, at))
    ]
    own = [[copy for copy, (b, _) in zip(copies, at) if b // held == unit] for unit in range(units)]
    loads = [
        pltpu.make_async_copy(src, dst, wsem.at[i])
        for i, (src, dst) in enumerate(((wg_hbm, wg), (wu_hbm, wu), (wd_hbm, wd)))
    ]
    for copy in own[0] + loads + sum(own[1:], []):
        copy.start()

    def tile(unit, base, first, take):
        slots = slot_ref[unit]
        slots_t = jnp.transpose(jnp.broadcast_to(slots, (128, tokens)))
        slot = lax.broadcasted_iota(jnp.int32, (take, tokens), 0).astype(F32) + base
        hit = slot == slots
        pick = jnp.where(hit, 1.0, 0.0).astype(BF16)
        gate = jnp.sum(jnp.where(hit, gate_ref[unit], 0.0), axis=1, keepdims=True)
        lane = lax.broadcasted_iota(jnp.int32, (tokens, 128), 1).astype(F32) + base
        put = jnp.concatenate(
            [jnp.where(lane + n == slots_t, 1.0, 0.0).astype(BF16) for n in range(0, take, 128)], axis=1
        )[:, :take]
        if first:
            for copy in own[unit]:
                copy.wait()
        at = slice(unit * tokens, (unit + 1) * tokens)
        for n in range(0, width, WIDE):
            cols = slice(n, n + WIDE)
            xg[:take, cols] = jnp.dot(pick, x_ref[at, cols], preferred_element_type=F32).astype(BF16)
        if first and unit == 0:
            loads[0].wait()
            loads[1].wait()
        g = jnp.dot(xg[:take], wg[...], preferred_element_type=F32)
        u = jnp.dot(xg[:take], wu[...], preferred_element_type=F32)
        hid[:take] = (g / (1.0 + jnp.exp(-g)) * u).astype(BF16)
        if first and unit == 0:
            loads[2].wait()
        for n in range(0, width, WIDE):
            cols = slice(n, n + WIDE)
            o = jnp.dot(hid[:take], wd[:, cols], preferred_element_type=F32).astype(BF16)
            o = (o.astype(F32) * gate).astype(BF16)
            back = jnp.dot(put, o, preferred_element_type=F32).astype(BF16)
            y_ref[at, cols] = back if first else y_ref[at, cols] + back

    sends = []
    for unit in range(units):
        tile(unit, 0.0, True, take)

        def more(i, carry):
            tile(unit, (take + i * REST).astype(F32), False, REST)
            return carry

        lax.fori_loop(0, lax.div(jnp.maximum(count_ref[unit] - take, 0) + (REST - 1), REST), more, 0)
        for b in range(unit * held, (unit + 1) * held):
            send = pltpu.make_async_copy(y_ref.at[b * span : (b + 1) * span], outs[b], osem.at[b])
            send.start()
            sends.append(send)
    for send in sends:
        send.wait()


def experts(count, slots, gate, pieces, wg, wu, wd, extra, size):
    at = [piece[:2] for piece in pieces]
    pieces = [piece[2] for piece in pieces]
    span, width = pieces[0].shape
    tokens = size * span
    take = slots.shape[2] * 7 // 16
    ratio = 2 * slots.shape[0]
    n = len(pieces)
    ff = wg.shape[1]
    return pl.pallas_call(
        functools.partial(expert_kernel, at=at, span=span, extras=len(extra), size=size),
        out_shape=(jax.ShapeDtypeStruct((span, width), BF16),) * size,
        in_specs=[spec(SMEM)] + [spec(VMEM)] * 2 + [spec(HBM)] * (n + 3 + len(extra)),
        out_specs=(spec(HBM),) * size,
        scratch_shapes=[
            VMEM((tokens, width), BF16),
            VMEM((tokens, width), BF16),
            VMEM(wg.shape, BF16),
            VMEM(wu.shape, BF16),
            VMEM(wd.shape, BF16),
            VMEM((take, width), BF16),
            VMEM((take, ff), BF16),
            pltpu.SemaphoreType.DMA((n,)),
            pltpu.SemaphoreType.DMA((3,)),
            pltpu.SemaphoreType.DMA((size,)),
        ],
        compiler_params=params(),
        cost_estimate=pl.CostEstimate(
            flops=ratio * (6 * take * width * ff + 4 * take * tokens * width), bytes_accessed=18 * MB, transcendentals=0
        ),
        name="experts",
    )(count, slots, gate, *pieces, wg, wu, wd, *extra)


def route(mine, size, groups):
    span = groups * mine.shape[1]
    units = 1
    while size * span // units > 1024:
        units *= 2
    mine = mine.reshape(units, -1)
    at = jnp.arange(mine.shape[1], dtype=jnp.int32)
    routed = mine > 0
    before = jnp.dot(routed.astype(BF16), (at[:, None] < at[None, :]).astype(BF16), preferred_element_type=F32)
    slots = jnp.where(routed, before, -1.0)
    return mine[:, None], slots[:, None], jnp.sum(routed.astype(jnp.int32), axis=1)


def by_gathers(tokens, gates_to_me, moe_gain, w_gate, w_up, w_down, groups, size, chunks, head_parts, late):
    z = lax.axis_index("req")
    resident = lax.dynamic_slice_in_dim(tokens, z * ROWS, ROWS, 0)
    starts = [sum(chunks[:c]) for c in range(len(chunks))]
    number = len(chunks)
    kept, stacks = [], []

    def settle(c, parts, extra=()):
        rows = resident[starts[c] : starts[c] + chunks[c]]
        after, moe_in = add_norm(rows, moe_gain[None], along_sum(parts, z, groups), extra)
        kept.append(after)
        stacks.append(along_gather(moe_in, z, groups))
        return moe_in

    for c in range(number):
        extra = [] if c == 0 else [parts[0]]
        if c >= 2:
            settle(c - 2, waiting)
            extra += [stacks[c - 2]]
        if c >= 1:
            waiting = parts
        parts, marks = head_parts(c, extra)
        if c == 0:
            near_e = jnp.arange(size, dtype=jnp.int32)[:, None] ^ marks[1]
            far = (marks[2] - jnp.array(ORDER, jnp.int32)[None]) % groups
            near_first = gates_to_me[(far * size + near_e).reshape(-1)]
    settle(number - 2, waiting, [parts[0]])
    routed_to_me = [route(near_first[:, starts[c] : starts[c] + rows], size, groups) for c, rows in enumerate(chunks)]
    appended = late([kept[0]] + [v for group in routed_to_me for v in group])
    settle(number - 1, parts, appended)

    near, results, both, out = [], [], [None] * number, [None] * number
    sides, corners = [], []
    near.append(neighbours(stacks[0], size))

    def finish(c):
        rows = chunks[c]
        terms = both[c][0] + sides[c]
        cut = {k: add(*(term[i * rows : (i + 1) * rows] for term in terms)) for i, k in enumerate(ORDER)}
        parts = [cut[0]] + [shift(cut[k], -k, groups) for k in (2, 1, 3)]
        return add(kept[c], *parts)

    for c, rows in enumerate(chunks):
        mine, slots, count = routed_to_me[c]
        x, y = near[c]
        pieces = siblings(listed(stacks[c], x, y, *relays(x, y, size)), size)
        extra = []
        if c == 0:
            extra += list(appended)
        else:
            extra += list(corners[c - 1])
        if c + 1 < number:
            extra += [stacks[c + 1]]
            near.append(neighbours(stacks[c + 1], size))
        made = experts(count, slots, mine, pieces, w_gate, w_up, w_down, extra, size)
        deps = []
        if c + 1 < number:
            deps += list(near[c + 1])
        if c > 0:
            sides.append(beside(both[c - 1], *corners[c - 1], size))
            deps += list(sides[c - 1])
        made = tie(made, deps) if deps else made
        both[c] = paired(made, size)
        corners.append(corner(both[c], size))
        if c > 0:
            results.append(finish(c - 1))
    sides.append(beside(both[-1], *corners[-1], size))
    results.append(finish(number - 1))
    return jnp.concatenate(results), appended


def by_all_to_all(routes, gates, after_attn, moe_in, w_gate, w_up, w_down, experts_n):
    row_count, model_width = moe_in.shape
    top_k = routes.shape[1]
    capacity = 3 * top_k * row_count // (2 * experts_n)
    flat_ids = routes.reshape(-1)
    onehot = (flat_ids[:, None] == jnp.arange(experts_n, dtype=jnp.int32)[None, :]).astype(jnp.int32)
    slots = jnp.sum((jnp.cumsum(onehot, axis=0) - 1) * onehot, axis=1)
    target = flat_ids * capacity + slots
    sources = jnp.arange(row_count * top_k, dtype=jnp.int32) // top_k
    outgoing = jnp.zeros((experts_n * capacity, model_width), BF16).at[target].set(moe_in[sources])
    outgoing = outgoing.reshape(experts_n, capacity, model_width)
    block_in = lax.all_to_all(outgoing, ("req", "exp"), split_axis=0, concat_axis=0, tiled=True)
    flat_rows = block_in.reshape(-1, model_width)
    gate_proj = jnp.dot(flat_rows, w_gate, preferred_element_type=F32)
    up_proj = jnp.dot(flat_rows, w_up, preferred_element_type=F32)
    activated = (jax.nn.silu(gate_proj) * up_proj).astype(BF16)
    produced = jnp.dot(activated, w_down, preferred_element_type=F32).astype(BF16)
    returned = lax.all_to_all(
        produced.reshape(block_in.shape), ("req", "exp"), split_axis=0, concat_axis=0, tiled=True
    )
    picked = returned.reshape(experts_n * capacity, model_width)[target].reshape(row_count, top_k, model_width)
    combined = jnp.sum(picked.astype(F32) * gates[:, :, None], axis=1)
    return (after_attn.astype(F32) + combined).astype(BF16)


def append_kernel(marks, kc_ref, vc_ref, kn_ref, vn_ref, *rest):
    k_out, v_out, k_all, v_all, sem = rest[-5:]
    ctx, hd = kc_ref.shape
    fresh = kn_ref.shape[0]
    length = marks[0]
    base = pl.multiple_of(lax.div(length, 16) * 16, 16)
    window = fresh + 16
    kept = lax.broadcasted_iota(jnp.int32, (ctx, hd), 0) < length
    row = lax.broadcasted_iota(jnp.int32, (window, fresh), 0) - (length - base)
    move = jnp.where(row == lax.broadcasted_iota(jnp.int32, (window, fresh), 1), 1.0, 0.0).astype(BF16)
    old = lax.broadcasted_iota(jnp.int32, (window, hd), 0) < length - base
    copies = []
    sides = ((kc_ref, kn_ref, k_all, k_out), (vc_ref, vn_ref, v_all, v_out))
    for i, (cache, new, whole, out) in enumerate(sides):
        whole[:ctx] = jnp.where(kept, cache[...].astype(F32), 0.0).astype(BF16)
        whole[ctx:] = jnp.zeros((whole.shape[0] - ctx, hd), BF16)
        added = jnp.dot(move, new[...], preferred_element_type=F32)
        at = pl.ds(base, window)
        whole[at] = jnp.where(old, whole[at].astype(F32), added).astype(BF16)
        copy = pltpu.make_async_copy(whole.at[: ctx + fresh], out, sem.at[i])
        copy.start()
        copies.append(copy)
    for copy in copies:
        copy.wait()


def append(marks, kc, vc, kn, vn, extra=()):
    rows, hd = kc.shape[0] + kn.shape[0], kc.shape[1]
    shape = jax.ShapeDtypeStruct((rows, hd), BF16)
    return pl.pallas_call(
        append_kernel,
        out_shape=(shape, shape),
        in_specs=[spec(SMEM)] + [spec(VMEM)] * 4 + [spec(HBM)] * len(extra),
        out_specs=(spec(HBM),) * 2,
        scratch_shapes=[VMEM((rows + 16, hd), BF16), VMEM((rows + 16, hd), BF16), pltpu.SemaphoreType.DMA((2,))],
        compiler_params=params(),
        cost_estimate=pl.CostEstimate(flops=0, bytes_accessed=5 * MB, transcendentals=0),
        name="append",
    )(marks, kc, vc, kn, vn, *extra)


def body(
    hidden_in,
    cache_keys,
    cache_values,
    cache_len,
    attn_gain,
    w_query,
    w_key,
    w_value,
    q_gain,
    k_gain,
    w_out,
    moe_gain,
    expert_ids,
    expert_gates,
    w_gate,
    w_up,
    w_down,
):
    groups, size = lax.axis_size("req"), lax.axis_size("exp")
    z, e = lax.axis_index("req"), lax.axis_index("exp")
    small = groups == 4 and size == 8
    chunks = CHUNKS if small else (ROWS,)
    tokens = hidden_in[0]
    length = cache_len[0]
    hd = q_gain.shape[0]
    heads = w_query.shape[1] // hd
    marks = jnp.stack([length, e, z]).astype(jnp.int32)

    w_qkv = join(w_query, w_key, w_value)
    if small:
        x, y = neighbours(w_qkv, size)
        first, second = relays(x, y, size)
        qkv_pieces = siblings(listed(w_qkv, x, y, first, second), size)
        w_out = stage(w_out, [x, y])
        out_x, out_y = neighbours(w_out, size)
    else:
        qkv_pieces = spread(w_qkv, size)
        out_pieces = spread(w_out, size)

    if small:
        ids, gates = expert_ids[0], expert_gates[0]
        number = groups * size
        dense = jnp.sum(
            jnp.where(ids[:, :, None] == jnp.arange(number, dtype=jnp.int32), gates[:, :, None], 0.0), axis=1
        )
        gates_to_me = lax.all_to_all(dense.T, ("req", "exp"), split_axis=0, concat_axis=0, tiled=True)

    starts = [sum(chunks[:c]) for c in range(len(chunks))]

    def chunked(array):
        blocks = array.reshape((groups, ROWS) + array.shape[1:])
        parts = [
            blocks[:, at : at + rows].reshape((groups * rows,) + array.shape[1:]) for at, rows in zip(starts, chunks)
        ]
        return jnp.concatenate(parts)

    token_at = chunked(jnp.arange(tokens.shape[0], dtype=jnp.int32))
    frequency = THETA ** (-jnp.arange(hd // 2, dtype=F32) * 2.0 / hd)
    angles = (length + token_at).astype(F32)[:, None] * frequency[None, :]
    cosine, sine = jnp.cos(angles), jnp.sin(angles)
    *q, k_new, v_new = project(
        marks,
        chunked(tokens),
        attn_gain[None],
        jnp.concatenate([cosine, cosine], axis=1),
        jnp.concatenate([-sine, sine], axis=1),
        q_gain[None],
        k_gain[None],
        qkv_pieces,
        size,
        heads,
        chunks,
        groups,
        [gates_to_me] if small else [],
    )
    pieces = []

    def head_parts(c, extra):
        args = marks, q[c], cache_keys[0], cache_values[0], k_new, v_new, starts[c], chunks[c], heads, extra
        if c == 0:
            att, seen = attend(*args)
            pieces[:] = out_pieces(att) if small else out_pieces
            return out_project(marks, att, pieces, size, groups), seen
        *parts, seen = attend(*args, pieces, size, groups)
        return parts, seen

    if small:
        out_x, out_y = tie([out_x, out_y], [k_new])
        out_first, out_second = relays(out_x, out_y, size)

        def out_pieces(att):
            first, second = tie([out_first, out_second], [att])
            return siblings(listed(w_out, out_x, out_y, first, second), size)

    def late(extra):
        return append(marks, cache_keys[0], cache_values[0], k_new, v_new, extra)

    if small:
        result_rows, (keys_out, values_out) = by_gathers(
            tokens, gates_to_me, moe_gain, w_gate[0], w_up[0], w_down[0], groups, size, chunks, head_parts, late
        )
    else:
        resident = lax.dynamic_slice_in_dim(tokens, z * ROWS, ROWS, 0)
        parts = along_sum(head_parts(0, [])[0], z, groups)
        after, moe_in = add_norm(resident, moe_gain[None], parts)
        result_rows = by_all_to_all(
            expert_ids[0], expert_gates[0], after, moe_in, w_gate[0], w_up[0], w_down[0], groups * size
        )
        keys_out, values_out = late([after])
    return (result_rows[None], keys_out[None], values_out[None])


def solution(mesh):
    placed = (
        P("exp", None, None),
        P("exp", None, "req"),
        P("exp", None, "req"),
        P("exp"),
        P(),
        P("exp", "req"),
        P("exp", "req"),
        P("exp", "req"),
        P(),
        P(),
        P(("req", "exp"), None),
        P(),
        P("exp", "req", None),
        P("exp", "req", None),
        P(("req", "exp"), None, None),
        P(("req", "exp"), None, None),
        P(("req", "exp"), None, None),
    )
    return jax.shard_map(
        body,
        mesh=mesh,
        in_specs=placed,
        out_specs=(P("exp", "req", None), P("exp", None, "req"), P("exp", None, "req")),
        check_vma=False,
    )
```
